512 devices in a mesh: doc: 128 (over y, x_lo, z), term: 4 (over x_hi, core).
Axes of the slice: x: 4 (x_hi: 2, x_lo: 2; x = x_hi * 2 + x_lo), y: 4, z: 16, core: 2. Of those that a mesh axis runs over, the one named last changes fastest.
Arguments:
- tfidf: bfloat16 [4096, 131072], P('term', 'doc'), may hold values from 50 to 1000
- pattern: int32 [32, 1024], P('term', 'doc'), may hold values 0 or 1
- factor_w: bfloat16 [4096, 256], P('term'), may hold values from 0.29882812 to 3
- factor_h: bfloat16 [256, 131072], P(None, 'doc'), may hold values from 0.29882812 to 3
Outputs:
- updated_w: bfloat16 [4096, 256], P('term')
- updated_h: bfloat16 [256, 131072], P(None, 'doc')
The draws below stay inside these ranges and needn't reach their ends.
All inputs are finite; a program needn't handle non-finite values. No bound on the sum of `pattern` on one device may be relied on, other than what follows from the above.
Results may differ from the reference program's by a relative error of at most 0.0004.
The reference program's roundings to bfloat16 on the way count: a program that leaves them out, or rounds other values in their place, can miss the bound.
Values may be sent and summed in bfloat16 or wider, within the bound.
A program may use at most 64 MiB of HBM per device.

```python
import math
import jax
import jax.numpy as jnp
from jax import lax

K = 256
BLOCK = 128
DOC_DEV = 1024
TERMS = 4096
DOCS = 131072
TERM_BLOCKS = 32
DOC_BLOCKS = 1024
N_DOC = 128


def plant(drawn, stream_key, least, high):
    longest = drawn.shape.index(max(drawn.shape))
    spots = []
    for shift in (0, 1):
        where = [jax.random.randint(jax.random.fold_in(stream_key, axis), (), 0, length) for axis, length in enumerate(drawn.shape)]
        where[longest] = (where[longest] + shift) % drawn.shape[longest]
        spots.append(tuple(where))
    return drawn.at[spots[0]].set(least).at[spots[1]].set(high)


def block_scale(rng, extent, split, low, top_value):
    def one(position, blocks):
        steps = jax.random.uniform(jax.random.fold_in(jax.random.fold_in(rng, 6), position), (blocks,), jnp.float32, low / len(split), top_value / len(split))
        return jnp.repeat(jnp.exp(steps), extent[position] // blocks).reshape((-1,) + (1,) * (len(extent) - position - 1))

    level = one(*split[0])
    for cut in split[1:]:
        level = level * one(*cut)
    return level


def setup_inputs(seed: int = 0) -> dict:
    key_of = jax.random.split(jax.random.key(seed), 5)
    tfidf = jnp.clip(jnp.exp(math.log(1000.0) - 2.9957323 * jax.random.uniform(key_of[0], (TERMS, DOCS), jnp.float32) ** block_scale(key_of[0], (TERMS, DOCS), ((0, 4), (1, 128)), -0.2, 0.2)), 50.0, 1000.0).astype(jnp.bfloat16)
    pattern = plant((jax.random.randint(key_of[1], (TERM_BLOCKS, DOC_BLOCKS), 0, 4) < 3).astype(jnp.int32), jax.random.fold_in(key_of[1], 1), 0, 1)
    factor_w = jnp.clip(jnp.exp(math.log(3.0) - 2.306499 * jax.random.uniform(key_of[2], (TERMS, K), jnp.float32) ** block_scale(key_of[2], (TERMS, K), ((0, 4),), -0.2, 0.2)), 0.29882812, 3.0).astype(jnp.bfloat16)
    factor_h = jnp.clip(jnp.exp(math.log(3.0) - 2.306499 * jax.random.uniform(key_of[3], (K, DOCS), jnp.float32) ** block_scale(key_of[3], (K, DOCS), ((1, 128),), -0.2, 0.2)), 0.29882812, 3.0).astype(jnp.bfloat16)
    return dict(tfidf=tfidf, pattern=pattern, factor_w=factor_w, factor_h=factor_h)


def expand(pattern):
    block_rows, block_cols = pattern.shape
    spread = jnp.broadcast_to(pattern[:, None, :, None], (block_rows, BLOCK, block_cols, BLOCK))
    return spread.reshape(block_rows * BLOCK, block_cols * BLOCK)


def reference(tfidf, pattern, factor_w, factor_h):
    gram_w = jnp.dot(factor_w.T, factor_w, preferred_element_type=jnp.float32).astype(jnp.bfloat16)
    per_slab = DOC_DEV // BLOCK

    def visit(totals, slab_index):
        term_topic, gram_sum = totals
        first_col = (slab_index * DOC_DEV).astype(jnp.int32)
        doc_slab = lax.dynamic_slice_in_dim(tfidf, first_col, DOC_DEV, 1)
        slab_mask = expand(lax.dynamic_slice_in_dim(pattern, (slab_index * per_slab).astype(jnp.int32), per_slab, 1))
        doc_slab = doc_slab * slab_mask.astype(doc_slab.dtype)
        old_h = lax.dynamic_slice_in_dim(factor_h, first_col, DOC_DEV, 1)
        numerator = jnp.dot(factor_w.T, doc_slab, preferred_element_type=jnp.float32)
        denominator = jnp.dot(gram_w, old_h, preferred_element_type=jnp.float32)
        new_h = (old_h.astype(jnp.float32) * numerator / denominator).astype(jnp.bfloat16)
        term_topic = term_topic + jnp.dot(doc_slab, new_h.T, preferred_element_type=jnp.float32)
        gram_sum = gram_sum + jnp.dot(new_h, new_h.T, preferred_element_type=jnp.float32)
        return (term_topic, gram_sum), new_h

    start_totals = (jnp.zeros((TERMS, K), jnp.float32), jnp.zeros((K, K), jnp.float32))
    (term_topic, gram_sum), slabs = lax.scan(visit, start_totals, jnp.arange(N_DOC, dtype=jnp.int32))
    updated_h = jnp.transpose(slabs, (1, 0, 2)).reshape(K, DOCS)
    gram_h = gram_sum.astype(jnp.bfloat16)
    denominator = jnp.dot(factor_w, gram_h, preferred_element_type=jnp.float32)
    updated_w = (factor_w.astype(jnp.float32) * term_topic / denominator).astype(jnp.bfloat16)
    return (updated_w, updated_h)
```

```python
import jax
import jax.numpy as jnp
from jax import lax
from jax.experimental import pallas as pl
from jax.experimental.pallas import tpu as pltpu
from jax.sharding import PartitionSpec as P

K = 256
BLOCK = 128
NXY = 8
NZ = 16
MESH = pl.DeviceIdType.MESH
F32 = jnp.float32
BF16 = jnp.bfloat16
LEVELS = 65535.0


def dot_tt(a, b, dims):
    return lax.dot_general(a, b, ((dims[0], dims[1]), ((), ())), preferred_element_type=F32)


def encode(value, peak):
    inv = jnp.where(peak > 0.0, LEVELS / peak, 0.0)
    return ((value * inv + 0.5).astype(jnp.int32) - 32768).astype(jnp.int16)


def decode(code, step):
    return (code.astype(jnp.int32) + 32768).astype(F32) * step


def kernel(
    tf_hbm, pat_ref, w_hbm, h_hbm, outw_hbm, outh_hbm,
    tf, masked, w, h, neww, newh,
    hsend, hrecv, gsend, grecv,
    hcode, hcode_in, hstep, hstep_in, gcode, gcode_in, gstep, gstep_in,
    gram_w, gpart, gxy_in, gz, gz_in, gtile, gfull, gram_h,
    acc, wcode, wcode_in, wstep, wstep_in, zsum, zsum_in, znum, znum_in,
    local_sem, core_s, core_r, x2_s, x2_r, gxy_s, gxy_r, gz_s, gz_r, gt_s, gt_r, gf_s, gf_r,
    wc_s, wc_r, ws_s, ws_r, zs_s, zs_r, zn_s, zn_r, ow_s, ow_r,
):
    doc = lax.axis_index("doc")
    term = lax.axis_index("term")
    z = lax.rem(doc, NZ)
    q = lax.div(doc, NZ)
    xh = lax.div(term, 2)
    c = lax.rem(term, 2)
    oc = 1 - c

    def at_core():
        return {"doc": doc, "term": xh * 2 + oc}

    def at_x2():
        return {"doc": doc, "term": (1 - xh) * 2 + c}

    def at_term(t):
        return {"doc": doc, "term": t}

    def at_xy(p):
        return {"doc": p * NZ + z, "term": term}

    def at_z(p):
        return {"doc": q * NZ + p, "term": term}

    def remote(src, dst, ssem, rsem, device):
        return pltpu.make_async_remote_copy(
            src_ref=src, dst_ref=dst, send_sem=ssem, recv_sem=rsem, device_id=device, device_id_type=MESH
        )

    load_w = pltpu.make_async_copy(w_hbm, w, local_sem.at[0])
    load_tf = pltpu.make_async_copy(tf_hbm, tf, local_sem.at[1])
    load_h = pltpu.make_async_copy(h_hbm, h, local_sem.at[2])
    load_w.start()
    load_tf.start()
    load_h.start()

    barrier = pltpu.get_barrier_semaphore()
    for k in range(1, 4):
        pl.semaphore_signal(barrier, inc=1, device_id=at_term(lax.rem(term + k, 4)), device_id_type=MESH)
    for k in range(1, NXY):
        pl.semaphore_signal(barrier, inc=1, device_id=at_xy(lax.rem(q + k, NXY)), device_id_type=MESH)
    for k in range(1, NZ):
        pl.semaphore_signal(barrier, inc=1, device_id=at_z(lax.rem(z + k, NZ)), device_id_type=MESH)

    load_w.wait()
    wv = w[...]
    gsend[...] = dot_tt(wv, wv, ((0,), (0,))).reshape(2, 128, K)
    load_tf.wait()
    for i in range(8):
        for j in range(8):
            rows, cols = pl.ds(i * BLOCK, BLOCK), pl.ds((j % 4) * BLOCK, BLOCK)
            on = pat_ref[i, j].astype(F32).astype(BF16)
            masked[j // 4, rows, cols] = tf[rows, pl.ds(j * BLOCK, BLOCK)] * on

    hsend[...] = dot_tt(wv, masked[oc], ((0,), (0,)))

    pl.semaphore_wait(barrier, 3 + (NXY - 1) + (NZ - 1))
    sends = []

    g_copy = remote(gsend.at[oc], grecv, core_s.at[0], core_r.at[0], at_core())
    g_copy.start()
    h_copy = remote(hsend, hrecv, core_s.at[1], core_r.at[1], at_core())
    h_copy.start()
    own = dot_tt(wv, masked[c], ((0,), (0,)))

    g_copy.wait_recv()
    part = gsend[c] + grecv[...]
    peak = jnp.max(part, axis=0, keepdims=True)
    gstep[...] = peak / LEVELS
    gcode[...] = encode(part, peak)
    gx = remote(gcode, gcode_in, x2_s.at[0], x2_r.at[0], at_x2())
    gx.start()
    gsx = remote(gstep, gstep_in, x2_s.at[1], x2_r.at[1], at_x2())
    gsx.start()

    h_copy.wait_recv()
    part = own + hrecv[...]
    peak = jnp.max(part, axis=0, keepdims=True)
    hstep[...] = peak / LEVELS
    hcode[...] = encode(part, peak)
    hsx = remote(hstep, hstep_in, x2_s.at[2], x2_r.at[2], at_x2())
    hsx.start()
    hx = remote(hcode, hcode_in, x2_s.at[3], x2_r.at[3], at_x2())
    hx.start()
    sends += [g_copy, h_copy, gx, gsx, hsx, hx]

    gx.wait_recv()
    gsx.wait_recv()
    total = decode(gcode[...], gstep[...]) + decode(gcode_in[...], gstep_in[...])
    gram_w[c] = total.astype(BF16)
    gw_copy = remote(gram_w.at[c], gram_w.at[c], core_s.at[2], core_r.at[2], at_core())
    gw_copy.start()
    load_h.wait()
    gw_copy.wait_recv()
    hv = h[:, pl.ds(pl.multiple_of(c * 512, 512), 512)]
    den = jnp.dot(gram_w[...].reshape(K, K), hv, preferred_element_type=F32)
    hsx.wait_recv()
    hx.wait_recv()
    total = decode(hcode[...], hstep[...]) + decode(hcode_in[...], hstep_in[...])
    newh[c] = (hv.astype(F32) * total / den).astype(BF16)
    nh_copy = remote(newh.at[c], newh.at[c], core_s.at[3], core_r.at[3], at_core())
    nh_copy.start()
    sends += [gw_copy, nh_copy]
    nh_copy.wait_recv()
    store_h = [
        pltpu.make_async_copy(newh.at[i], outh_hbm.at[:, pl.ds(i * 512, 512)], local_sem.at[3 + i]) for i in range(2)
    ]
    for copy in store_h:
        copy.start()

    col = pl.ds(pl.multiple_of(c * 128, 128), 128)
    gpart[...] = dot_tt(newh[0], newh[0, col, :], ((1,), (1,))) + dot_tt(newh[1], newh[1, col, :], ((1,), (1,)))
    gxy = []
    for k in range(1, NXY):
        p = lax.rem(q + k, NXY)
        tile = pl.ds(pl.multiple_of(p * 32 + xh * 16, 16), 16)
        copy = remote(gpart.at[tile], gxy_in.at[q], gxy_s.at[k], gxy_r.at[q], at_xy(p))
        copy.start()
        gxy.append(copy)

    wc, ws = [], []
    for k in range(1, NXY):
        p = lax.rem(q + k, NXY)
        rows = pl.ds(pl.multiple_of(p * 128, 128), 128)
        value = dot_tt(masked[0, rows, :], newh[0], ((1,), (1,))) + dot_tt(masked[1, rows, :], newh[1], ((1,), (1,)))
        peak = jnp.max(value, axis=0, keepdims=True)
        code = encode(value, peak)
        step = peak / LEVELS
        for i in range(2):
            wcode[k, i] = code[:, i * 128 : (i + 1) * 128]
        wstep[k] = step
        cs = remote(wstep.at[k], wstep_in.at[q], ws_s.at[k], ws_r.at[q], at_xy(p))
        cs.start()
        ws.append(cs)
        cc = remote(wcode.at[k], wcode_in.at[q], wc_s.at[k], wc_r.at[q], at_xy(p))
        cc.start()
        wc.append(cc)
    rows = pl.ds(pl.multiple_of(q * 128, 128), 128)
    value = dot_tt(masked[0, rows, :], newh[0], ((1,), (1,))) + dot_tt(masked[1, rows, :], newh[1], ((1,), (1,)))
    acc[0] = value[:, :128]
    acc[1] = value[:, 128:]

    gsum = gpart[pl.ds(pl.multiple_of(q * 32 + xh * 16, 16), 16), :]
    for k in range(1, NXY):
        p = lax.rem(q + NXY - k, NXY)
        remote(gxy_in.at[p], gxy_in.at[p], gxy_s.at[k], gxy_r.at[p], at_xy(p)).wait_recv()
        gsum = gsum + gxy_in[p]
    gz[...] = gsum
    gz_in[z] = gsum
    gzc = []
    for k in (8, 7, 9, 6, 10, 5, 11, 4, 12, 3, 13, 2, 14, 1, 15):
        p = lax.rem(z + k, NZ)
        copy = remote(gz, gz_in.at[z], gz_s.at[k], gz_r.at[z], at_z(p))
        copy.start()
        gzc.append(copy)

    total = acc[...]
    for k in range(1, NXY):
        p = lax.rem(q + NXY - k, NXY)
        remote(wstep_in.at[p], wstep_in.at[p], ws_s.at[k], ws_r.at[p], at_xy(p)).wait_recv()
        remote(wcode_in.at[p], wcode_in.at[p], wc_s.at[k], wc_r.at[p], at_xy(p)).wait_recv()
        step = wstep_in[p]
        total = total + jnp.stack(
            [decode(wcode_in[p, i], step[:, i * 128 : (i + 1) * 128]) for i in range(2)]
        )
    zsum[...] = total.reshape(NZ, 16, 128)
    zsc = []
    for k in (8, 7, 9, 6, 10, 5, 11, 4, 12, 3, 13, 2, 14, 1, 15):
        p = lax.rem(z + k, NZ)
        copy = remote(zsum.at[p], zsum_in.at[z], zs_s.at[k], zs_r.at[z], at_z(p))
        copy.start()
        zsc.append(copy)
    zsum_in[z] = zsum[z]

    for k in range(1, NZ):
        p = lax.rem(z + k, NZ)
        remote(gz, gz_in.at[p], gz_s.at[k], gz_r.at[p], at_z(p)).wait_recv()
    gsum = gz_in[0]
    for p in range(1, NZ):
        gsum = gsum + gz_in[p]
    gtile[q] = gsum.astype(BF16)
    gtc = []
    for k in range(1, NXY):
        p = lax.rem(q + k, NXY)
        copy = remote(gtile.at[q], gtile.at[q], gt_s.at[k], gt_r.at[q], at_xy(p))
        copy.start()
        gtc.append(copy)

    for k in range(1, NZ):
        p = lax.rem(z + k, NZ)
        remote(zsum_in.at[p], zsum_in.at[p], zs_s.at[k], zs_r.at[p], at_z(p)).wait_recv()
    zs = zsum_in[0]
    for p in range(1, NZ):
        zs = zs + zsum_in[p]
    znum[...] = zs
    znc = []
    for k in (8, 7, 9, 6, 10, 5, 11, 4, 12, 3, 13, 2, 14, 1, 15):
        p = lax.rem(z + k, NZ)
        copy = remote(znum, znum_in.at[z], zn_s.at[k], zn_r.at[z], at_z(p))
        copy.start()
        znc.append(copy)
    znum_in[z] = zs

    for k in range(1, NXY):
        p = lax.rem(q + k, NXY)
        remote(gtile.at[p], gtile.at[p], gt_s.at[k], gt_r.at[p], at_xy(p)).wait_recv()
    gfull[term] = gtile[...]
    gfc = []
    for k in range(1, 4):
        t = lax.rem(term + k, 4)
        copy = remote(gtile, gfull.at[term], gf_s.at[k], gf_r.at[term], at_term(t))
        copy.start()
        gfc.append(copy)
    for k in range(1, 4):
        t = lax.rem(term + k, 4)
        remote(gtile, gfull.at[t], gf_s.at[k], gf_r.at[t], at_term(t)).wait_recv()
    for xi in range(2):
        for ci in range(2):
            for p in range(NXY):
                gram_h[pl.ds(p * 32 + xi * 16, 16), pl.ds(ci * 128, 128)] = gfull[xi * 2 + ci, p]
    wrows = w[rows, :]
    den = jnp.dot(wrows, gram_h[...], preferred_element_type=F32)
    scaled = wrows.astype(F32)

    for k in range(1, NZ):
        p = lax.rem(z + k, NZ)
        remote(znum, znum_in.at[p], zn_s.at[k], zn_r.at[p], at_z(p)).wait_recv()
    numer = znum_in[...].reshape(2, 128, 128)
    for i in range(2):
        cols = slice(i * 128, (i + 1) * 128)
        neww[rows, pl.ds(i * 128, 128)] = (scaled[:, cols] * numer[i] / den[:, cols]).astype(BF16)
    owc = []
    for k in range(1, NXY):
        p = lax.rem(q + k, NXY)
        copy = remote(neww.at[rows], neww.at[rows], ow_s.at[k], ow_r.at[q], at_xy(p))
        copy.start()
        owc.append(copy)
    for k in range(1, NXY):
        p = lax.rem(q + k, NXY)
        theirs = neww.at[pl.ds(pl.multiple_of(p * 128, 128), 128)]
        remote(theirs, theirs, ow_s.at[k], ow_r.at[p], at_xy(p)).wait_recv()
    store_w = pltpu.make_async_copy(neww, outw_hbm, local_sem.at[5])
    store_w.start()
    for copy in sends + gxy + ws + wc + gzc + zsc + gtc + znc + gfc + owc:
        copy.wait_send()
    for copy in store_h:
        copy.wait()
    store_w.wait()


def on_device(tfidf, pattern, factor_w, factor_h):
    V = pltpu.VMEM
    i16 = jnp.int16
    scratch = [
        V((1024, 1024), BF16), V((2, 1024, 512), BF16), V((1024, K), BF16), V((K, 1024), BF16),
        V((1024, K), BF16), V((2, K, 512), BF16),
        V((K, 512), F32), V((K, 512), F32), V((2, 128, K), F32), V((128, K), F32),
        V((K, 512), i16), V((K, 512), i16), V((1, 512), F32), V((1, 512), F32),
        V((128, K), i16), V((128, K), i16), V((1, K), F32), V((1, K), F32),
        V((2, 128, K), BF16), V((K, 128), F32), V((NXY, 16, 128), F32), V((16, 128), F32), V((NZ, 16, 128), F32),
        V((NXY, 16, 128), BF16), V((4, NXY, 16, 128), BF16), V((K, K), BF16),
        V((2, 128, 128), F32), V((NXY, 2, 128, 128), i16), V((NXY, 2, 128, 128), i16),
        V((NXY, 1, K), F32), V((NXY, 1, K), F32),
        V((NZ, 16, 128), F32), V((NZ, 16, 128), F32), V((16, 128), F32), V((NZ, 16, 128), F32),
    ]
    D = pltpu.SemaphoreType.DMA
    sems = [D((6,)), D((4,)), D((4,)), D((4,)), D((4,))]
    for n in (NXY, NZ, NXY, 4, NXY, NXY, NZ, NZ, NXY):
        sems += [D((n,)), D((n,))]
    any_space = pl.BlockSpec(memory_space=pl.ANY)
    return pl.pallas_call(
        kernel,
        out_shape=(jax.ShapeDtypeStruct((1024, K), BF16), jax.ShapeDtypeStruct((K, 1024), BF16)),
        in_specs=[any_space, pl.BlockSpec(memory_space=pltpu.SMEM), any_space, any_space],
        out_specs=(any_space, any_space),
        scratch_shapes=scratch + sems,
        compiler_params=pltpu.CompilerParams(
            collective_id=0, has_side_effects=True, vmem_limit_bytes=48 * 1024 * 1024
        ),
    )(tfidf, pattern, factor_w, factor_h)


def solution(mesh):
    placed = (P("term", "doc"), P("term", "doc"), P("term", None), P(None, "doc"))
    return jax.shard_map(
        on_device,
        mesh=mesh,
        in_specs=placed,
        out_specs=(P("term", None), P(None, "doc")),
        check_vma=False,
    )
```

```python
import jax
import jax.numpy as jnp
from jax import lax
from jax.experimental import pallas as pl
from jax.experimental.pallas import tpu as pltpu
from jax.sharding import PartitionSpec as P

K = 256
BLOCK = 128
NXY = 8
NZ = 16
MESH = pl.DeviceIdType.MESH
F32 = jnp.float32
BF16 = jnp.bfloat16
I16 = jnp.int16
LEVELS = 65535.0
XY = ((2, 1), (2, 0), (1, 1), (3, 1), (1, 0), (3, 0), (0, 1))
ZS = (8, 7, 9, 6, 10, 5, 11, 4, 12, 3, 13, 2, 14, 1, 15)
NEAR = 9


def dot(a, b, dims):
    return lax.dot_general(a, b, (dims, ((), ())), preferred_element_type=F32)


def encode(value, peak):
    inv = jnp.where(peak > 0.0, LEVELS / peak, 0.0)
    return ((value * inv + 0.5).astype(jnp.int32) - 32768).astype(I16)


def decode(code, step):
    return (code.astype(jnp.int32) + 32768).astype(F32) * step


def kernel(
    tf_hbm, pat_hbm, w_hbm, h_hbm, outw, outh,
    tf, masked, pat, w, wt, h, newh, newht,
    hsend, hrecv, hcode, hcode_in, hstep, hstep_in,
    gsend, grecv, gcode, gcode_in, gstep, gstep_in, gram_w,
    gpart, gxy_in, gz, gz_in, gfull, gram_h, ratio,
    wcode, wcode_in, wstep, wstep_in, own_rel, zsum, zsum_in, znum_in, tiles,
    ready1, ready2,
    load_s, store_s, core_s, core_r, x2_s, x2_r, gxy_s, gxy_r, gz_s, gz_r, gf_s, gf_r,
    wf_s, wf_r, wn_s, wn_r, ws_s, ws_r, zs_s, zs_r, zn_s, zn_r, on_s, on_r, of_s, of_r,
):
    doc = lax.axis_index("doc")
    term = lax.axis_index("term")
    z = lax.rem(doc, NZ)
    q = lax.div(doc, NZ)
    y, xl = lax.div(q, 2), lax.rem(q, 2)
    xh = lax.div(term, 2)
    c = lax.rem(term, 2)
    oc = 1 - c

    def at_term(t):
        return {"doc": doc, "term": t}

    def xy_of(off, sign=1):
        return lax.rem(y + 4 + sign * off[0], 4) * 2 + lax.rem(xl + off[1], 2)

    def at_xy(p):
        return {"doc": p * NZ + z, "term": term}

    def at_z(k):
        return {"doc": q * NZ + lax.rem(z + k + NZ, NZ), "term": term}

    core = at_term(xh * 2 + oc)
    across = at_term((1 - xh) * 2 + c)
    sends = []

    def remote(src, dst, ssem, rsem, device):
        return pltpu.make_async_remote_copy(
            src_ref=src, dst_ref=dst, send_sem=ssem, recv_sem=rsem, device_id=device, device_id_type=MESH
        )

    def send(src, dst, ssem, rsem, device):
        copy = remote(src, dst, ssem, rsem, device)
        copy.start()
        sends.append(copy)
        return copy

    chunks = [oc * 2, oc * 2 + 1, c * 2, c * 2 + 1]
    cols = [pl.ds(pl.multiple_of(g * 256, 256), 256) for g in chunks]
    load_w = pltpu.make_async_copy(w_hbm, w, load_s.at[0])
    load_pat = pltpu.make_async_copy(pat_hbm, pat, load_s.at[1])
    load_h = pltpu.make_async_copy(h_hbm, h, load_s.at[2])
    load_tf = [pltpu.make_async_copy(tf_hbm.at[:, cols[i]], tf.at[:, cols[i]], load_s.at[3 + i]) for i in range(4)]
    load_w.start()
    load_pat.start()
    for copy in load_tf:
        copy.start()
    load_h.start()

    barrier = pltpu.get_barrier_semaphore()
    for off in ((0, 0),) + XY:
        for t in range(4):
            if off != (0, 0) or t:
                pl.semaphore_signal(
                    barrier, inc=1, device_id={"doc": xy_of(off) * NZ + z, "term": lax.rem(term + t, 4)}, device_id_type=MESH
                )
    for k in (-2, 2, -1, 1):
        pl.semaphore_signal(barrier, inc=1, device_id=at_z(k), device_id_type=MESH)

    load_w.wait()
    wt[...] = w[...].T
    gsend[...] = dot(wt[...], w[...], ((1,), (0,))).reshape(2, 128, K)
    load_pat.wait()

    def mask(i):
        load_tf[i].wait()
        for a in range(8):
            for b in range(2):
                rows = pl.ds(a * BLOCK, BLOCK)
                at = pl.ds(pl.multiple_of(chunks[i] * 256 + b * BLOCK, BLOCK), BLOCK)
                on = pat[a, chunks[i] * 2 + b].astype(F32).astype(BF16)
                masked[rows, at] = tf[rows, at] * on

    def numerator_h(i):
        return dot(wt[...], masked[:, cols[i]], ((1,), (0,)))

    mask(0)
    hsend[0] = numerator_h(0)
    pl.semaphore_wait(barrier, 35)
    for k in (-2, 2):
        pl.semaphore_signal(ready1, inc=1, device_id=at_z(k), device_id_type=MESH)

    g_copy = send(gsend.at[oc], grecv, core_s.at[0], core_r.at[0], core)
    h_copy = [send(hsend.at[0], hrecv.at[0], core_s.at[1], core_r.at[1], core)]
    mask(1)
    hsend[1] = numerator_h(1)
    h_copy.append(send(hsend.at[1], hrecv.at[1], core_s.at[2], core_r.at[2], core))

    g_copy.wait_recv()
    part = gsend[c] + grecv[...]
    peak = jnp.max(part, axis=0, keepdims=True)
    gstep[...] = peak / LEVELS
    gcode[...] = encode(part, peak)
    gx = [
        send(gcode, gcode_in, x2_s.at[0], x2_r.at[0], across),
        send(gstep, gstep_in, x2_s.at[1], x2_r.at[1], across),
    ]
    hx = []
    for u in range(2):
        mask(2 + u)
        own = numerator_h(2 + u)
        h_copy[u].wait_recv()
        part = own + hrecv[u]
        peak = jnp.max(part, axis=0, keepdims=True)
        hstep[u] = peak / LEVELS
        hcode[u] = encode(part, peak)
        hx.append(send(hstep.at[u], hstep_in.at[u], x2_s.at[2 + u], x2_r.at[2 + u], across))
        hx.append(send(hcode.at[u], hcode_in.at[u], x2_s.at[4 + u], x2_r.at[4 + u], across))

    for copy in gx:
        copy.wait_recv()
    total = decode(gcode[...], gstep[...]) + decode(gcode_in[...], gstep_in[...])
    gram_w[c] = total.astype(BF16)
    gw = send(gram_w.at[c], gram_w.at[c], core_s.at[3], core_r.at[3], core)
    pl.semaphore_wait(ready1, 2)
    for k in (-4, 4):
        pl.semaphore_signal(ready2, inc=1, device_id=at_z(k), device_id_type=MESH)
    load_h.wait()
    gw.wait_recv()
    stores = []
    nh = []
    for u in range(2):
        hv = h[:, cols[2 + u]]
        den = dot(gram_w[...].reshape(K, K), hv, ((1,), (0,)))
        hx[2 * u].wait_recv()
        hx[2 * u + 1].wait_recv()
        total = decode(hcode[u], hstep[u]) + decode(hcode_in[u], hstep_in[u])
        new = (hv.astype(F32) * total / den).astype(BF16)
        g = chunks[2 + u]
        newh[g] = new
        nh.append(send(newh.at[g], newh.at[g], core_s.at[4 + u], core_r.at[4 + u], core))
        stores.append(pltpu.make_async_copy(newh.at[g], outh.at[:, cols[2 + u]], store_s.at[u]))
        newht[pl.ds(pl.multiple_of(g * 256, 256), 256), :] = new.T

    rows = pl.ds(pl.multiple_of(xh * 128, 128), 128)
    for i in range(2):
        gpart[i] = sum(
            dot(newh[chunks[2 + u], rows, :], newht[pl.ds(pl.multiple_of(chunks[2 + u] * 256, 256), 256), i * 128 : i * 128 + 128], ((1,), (0,)))
            for u in range(2)
        )
    gxy = []
    n = 0
    for off in XY + ((0, 0),):
        p = xy_of(off)
        for dc in range(2):
            if off == (0, 0) and dc == 0:
                continue
            tc = lax.rem(c + dc, 2)
            tile = gpart.at[tc, pl.ds(pl.multiple_of(p * 16, 16), 16)]
            gxy.append(
                send(tile, gxy_in.at[n], gxy_s.at[n], gxy_r.at[n], {"doc": p * NZ + z, "term": xh * 2 + tc})
            )
            n += 1

    for u in range(2):
        g = chunks[u]
        theirs = newh.at[g]
        remote(theirs, theirs, core_s.at[4 + u], core_r.at[4 + u], core).wait_recv()
        newht[pl.ds(pl.multiple_of(g * 256, 256), 256), :] = newh[g].T
        stores.append(pltpu.make_async_copy(theirs, outh.at[:, cols[u]], store_s.at[2 + u]))

    def slot_of(tile):
        return lax.rem(tile + 20 - z, NZ)

    def part_of(p):
        return dot(masked[pl.ds(pl.multiple_of(p * 128, 128), 128), :], newht[...], ((1,), (0,)))

    wf, wn, ws = [], [], []
    for k, off in enumerate(XY):
        p = xy_of(off)
        value = part_of(p)
        peak = jnp.max(value, axis=0, keepdims=True)
        code = encode(value, peak)
        step = peak / LEVELS
        for i in range(2):
            wstep[k, i] = step[:, i * 128 : (i + 1) * 128]
            for b in range(8):
                wcode[k, slot_of(i * 8 + b)] = code[b * 16 : (b + 1) * 16, i * 128 : (i + 1) * 128]
        ws.append(send(wstep.at[k], wstep_in.at[k], ws_s.at[k], ws_r.at[k], at_xy(p)))
        wf.append(send(wcode.at[k, NEAR:], wcode_in.at[k, NEAR:], wf_s.at[k], wf_r.at[k], at_xy(p)))
    for k, off in enumerate(XY):
        wn.append(send(wcode.at[k, :NEAR], wcode_in.at[k, :NEAR], wn_s.at[k], wn_r.at[k], at_xy(xy_of(off))))
    value = part_of(q)
    for i in range(2):
        for b in range(8):
            own_rel[slot_of(i * 8 + b)] = value[b * 16 : (b + 1) * 16, i * 128 : (i + 1) * 128]
    for copy in stores:
        copy.start()

    gsum = gpart[c, pl.ds(pl.multiple_of(q * 16, 16), 16), :]
    for n in range(15):
        gxy[n].wait_recv()
        gsum = gsum + gxy_in[n]
    gz[...] = gsum
    gz_in[z] = gsum
    pl.semaphore_wait(ready2, 2)
    for k in ZS:
        send(gz, gz_in.at[z], gz_s.at[k], gz_r.at[z], at_z(k))

    def sum_xy(slots):
        for s in slots:
            half = lax.div(lax.rem(z + s + 12, NZ), 8)
            total = own_rel[s]
            for k in range(7):
                total = total + decode(wcode_in[k, s], wstep_in[k, half])
            zsum[s] = total

    zs = {}
    for k in range(7):
        ws[k].wait_recv()
        wf[k].wait_recv()
    sum_xy(range(NEAR, NZ))
    for k in ZS[:7]:
        s = (k + 4) % NZ
        zs[s] = send(zsum.at[s], zsum_in.at[s], zs_s.at[s], zs_r.at[s], at_z(k))
    for k in range(7):
        wn[k].wait_recv()
    sum_xy(range(NEAR))
    for k in ZS[7:]:
        s = (k + 4) % NZ
        zs[s] = send(zsum.at[s], zsum_in.at[s], zs_s.at[s], zs_r.at[s], at_z(k))

    for k in range(1, NZ):
        p = lax.rem(z + k, NZ)
        remote(gz, gz_in.at[p], gz_s.at[k], gz_r.at[p], at_z(k)).wait_recv()
    gsum = gz_in[0]
    for p in range(1, NZ):
        gsum = gsum + gz_in[p]
    mine = (xh * NXY + q) * 2 + c
    gfull[mine] = gsum.astype(BF16)
    gf = []
    n = 0
    for off in XY + ((0, 0),):
        p = xy_of(off)
        for dt in (2, 3, 1, 0):
            if off == (0, 0) and dt == 0:
                continue
            device = {"doc": p * NZ + z, "term": lax.rem(term + dt, 4)}
            send(gfull.at[mine], gfull.at[mine], gf_s.at[n], gf_r.at[mine], device)
            n += 1

    total = zsum[4]
    for s in range(NZ):
        if s != 4:
            zs[s].wait_recv()
            total = total + zsum_in[s]
    znum_in[4] = total
    zn = {}
    for k in ZS:
        s = (4 - k) % NZ
        zn[s] = send(znum_in.at[4], znum_in.at[s], zn_s.at[s], zn_r.at[s], at_z(k))

    for off in XY + ((0, 0),):
        p = xy_of(off)
        for dt in (2, 3, 1, 0):
            if off == (0, 0) and dt == 0:
                continue
            t = lax.rem(term + dt, 4)
            at = (lax.div(t, 2) * NXY + p) * 2 + lax.rem(t, 2)
            theirs = gfull.at[at]
            remote(theirs, theirs, gf_s.at[0], gf_r.at[at], at_term(t)).wait_recv()
    for a in range(16):
        for i in range(2):
            gram_h[pl.ds(a * 16, 16), pl.ds(i * 128, 128)] = gfull[a * 2 + i]
    wrows = w[pl.ds(pl.multiple_of(q * 128, 128), 128), :]
    ratio[...] = wrows.astype(F32) / dot(wrows, gram_h[...], ((1,), (0,)))

    def spot(s):
        tile = lax.rem(z + s + 12, NZ)
        return pl.multiple_of(lax.rem(tile, 8) * 16, 16), pl.multiple_of(lax.div(tile, 8) * 128, 128)

    def finish(slots):
        for s in slots:
            row, col = spot(s)
            tiles[q, s] = (ratio[pl.ds(row, 16), pl.ds(col, 128)] * znum_in[s]).astype(BF16)

    for s in range(NEAR):
        if s != 4:
            zn[s].wait_recv()
    finish(range(NEAR))
    on, of = [], []
    for k, off in enumerate(XY):
        src = tiles.at[q, :NEAR]
        on.append(send(src, src, on_s.at[k], on_r.at[q], at_xy(xy_of(off))))
    for s in range(NEAR, NZ):
        zn[s].wait_recv()
    finish(range(NEAR, NZ))
    for k, off in enumerate(XY):
        src = tiles.at[q, NEAR:]
        of.append(send(src, src, of_s.at[k], of_r.at[q], at_xy(xy_of(off))))

    def place(p, slots):
        for s in slots:
            row, col = spot(s)
            outw[pl.ds(pl.multiple_of(p * 128 + row, 16), 16), pl.ds(col, 128)] = tiles[p, s]

    place(q, range(NZ))
    for k, off in enumerate(XY):
        p = xy_of(off)
        theirs = tiles.at[p, :NEAR]
        remote(theirs, theirs, on_s.at[k], on_r.at[p], at_xy(p)).wait_recv()
        place(p, range(NEAR))
    for k, off in enumerate(XY):
        p = xy_of(off)
        theirs = tiles.at[p, NEAR:]
        remote(theirs, theirs, of_s.at[k], of_r.at[p], at_xy(p)).wait_recv()
        place(p, range(NEAR, NZ))
    for copy in sends:
        copy.wait_send()
    for copy in stores:
        copy.wait()


def on_device(tfidf, pattern, factor_w, factor_h):
    V = pltpu.VMEM
    scratch = [
        V((1024, 1024), BF16), V((1024, 1024), BF16), pltpu.SMEM((8, 8), jnp.int32),
        V((1024, K), BF16), V((K, 1024), BF16), V((K, 1024), BF16), V((4, K, 256), BF16), V((1024, K), BF16),
        V((2, K, 256), F32), V((2, K, 256), F32), V((2, K, 256), I16), V((2, K, 256), I16),
        V((2, 1, 256), F32), V((2, 1, 256), F32),
        V((2, 128, K), F32), V((128, K), F32), V((128, K), I16), V((128, K), I16), V((1, K), F32), V((1, K), F32),
        V((2, 128, K), BF16),
        V((2, 128, 128), F32), V((15, 16, 128), F32), V((16, 128), F32), V((NZ, 16, 128), F32),
        V((32, 16, 128), BF16), V((K, K), BF16), V((128, K), F32),
        V((7, NZ, 16, 128), I16), V((7, NZ, 16, 128), I16), V((7, 2, 1, 128), F32), V((7, 2, 1, 128), F32),
        V((NZ, 16, 128), F32), V((NZ, 16, 128), F32), V((NZ, 16, 128), F32), V((NZ, 16, 128), F32),
        V((NXY, NZ, 16, 128), BF16),
    ]
    D = pltpu.SemaphoreType.DMA
    sems = [pltpu.SemaphoreType.REGULAR, pltpu.SemaphoreType.REGULAR, D((7,)), D((4,))]
    for a, b in ((6, 6), (6, 6), (15, 15), (NZ, NZ), (31, 32), (7, 7), (7, 7), (7, 7), (NZ, NZ), (NZ, NZ), (7, 8), (7, 8)):
        sems += [D((a,)), D((b,))]
    hbm = pl.BlockSpec(memory_space=pltpu.HBM)
    return pl.pallas_call(
        kernel,
        out_shape=(jax.ShapeDtypeStruct((1024, K), BF16), jax.ShapeDtypeStruct((K, 1024), BF16)),
        in_specs=[hbm] * 4,
        out_specs=(pl.BlockSpec(memory_space=pltpu.VMEM), pl.BlockSpec(memory_space=pl.ANY)),
        scratch_shapes=scratch + sems,
        compiler_params=pltpu.CompilerParams(
            collective_id=0, has_side_effects=True, vmem_limit_bytes=32 * 1024 * 1024
        ),
    )(*(pltpu.with_memory_space_constraint(a, pltpu.HBM) for a in (tfidf, pattern, factor_w, factor_h)))


def solution(mesh):
    placed = (P("term", "doc"), P("term", "doc"), P("term", None), P(None, "doc"))
    return jax.shard_map(
        on_device,
        mesh=mesh,
        in_specs=placed,
        out_specs=(P("term", None), P(None, "doc")),
        check_vma=False,
    )
```

```python
import jax
import jax.numpy as jnp
from jax import lax
from jax.experimental import pallas as pl
from jax.experimental.pallas import tpu as pltpu
from jax.sharding import PartitionSpec as P

K = 256
BLOCK = 128
NXY = 8
NZ = 16
MESH = pl.DeviceIdType.MESH
F32 = jnp.float32
BF16 = jnp.bfloat16
I16 = jnp.int16
LEVELS = 65535.0
XY = ((2, 1), (2, 0), (1, 1), (3, 1), (1, 0), (3, 0), (0, 1))
ZS = (8, 7, 9, 6, 10, 5, 11, 4, 12, 3, 13, 2, 14, 1, 15)
NEAR = 9


def dot(a, b, dims):
    return lax.dot_general(a, b, (dims, ((), ())), preferred_element_type=F32)


def encode(value, peak):
    inv = jnp.where(peak > 0.0, LEVELS / peak, 0.0)
    return ((value * inv + 0.5).astype(jnp.int32) - 32768).astype(I16)


def decode(code, step):
    return (code.astype(jnp.int32) + 32768).astype(F32) * step


def kernel(
    tf_hbm, pat_hbm, w_hbm, h_hbm, outw, outh,
    tf, masked, pat, w, wt, h, newh, newht,
    hsend, hrecv, hcode, hcode_in, hstep, hstep_in,
    gsend, grecv, gcode, gcode_in, gstep, gstep_in, gram_w,
    gpart, gxy_in, gz, gz_in, gfull, gram_h, ratio,
    wcode, wcode_in, wstep, wstep_in, acc, zsum, zsum_in, znum_in, tiles,
    ready1, ready2,
    load_s, store_s, core_s, core_r, x2_s, x2_r, gxy_s, gxy_r, gz_s, gz_r, gf_s, gf_r,
    wf_s, wf_r, wn_s, wn_r, ws_s, ws_r, zs_s, zs_r, zn_s, zn_r, on_s, on_r, of_s, of_r,
):
    doc = lax.axis_index("doc")
    term = lax.axis_index("term")
    z = lax.rem(doc, NZ)
    q = lax.div(doc, NZ)
    y, xl = lax.div(q, 2), lax.rem(q, 2)
    xh = lax.div(term, 2)
    c = lax.rem(term, 2)
    oc = 1 - c

    def at_term(t):
        return {"doc": doc, "term": t}

    y_at = [lax.rem(y + i, 4) * 2 for i in range(4)]
    x_at = [xl, 1 - xl]
    xy_at = {off: y_at[off[0]] + x_at[off[1]] for off in ((0, 0),) + XY}
    z_at = [z] + [lax.rem(z + k, NZ) for k in range(1, NZ)]
    tile_at = [lax.rem(z + s + 12, NZ) for s in range(NZ)]
    half_at = [lax.div(tile, 8) for tile in tile_at]
    row_at = [lax.rem(tile, 8) * 16 for tile in tile_at]
    slot_at = [lax.rem(tile + 20 - z, NZ) for tile in range(NZ)]

    def xy_of(off):
        return xy_at[off]

    def at_xy(p):
        return {"doc": p * NZ + z, "term": term}

    def at_z(k):
        return {"doc": q * NZ + z_at[k % NZ], "term": term}

    term_at = [term] + [lax.rem(term + k, 4) for k in range(1, 4)]
    spread_at = [lax.div(t, 2) * (2 * NXY) + lax.rem(t, 2) for t in term_at]
    gram_at = {(i, dt): xy_at[off] * 2 + spread_at[dt] for i, off in enumerate(XY + ((0, 0),)) for dt in range(4)}
    mine = gram_at[len(XY), 0]

    core = at_term(xh * 2 + oc)
    across = at_term((1 - xh) * 2 + c)
    sends = []

    def remote(src, dst, ssem, rsem, device):
        return pltpu.make_async_remote_copy(
            src_ref=src, dst_ref=dst, send_sem=ssem, recv_sem=rsem, device_id=device, device_id_type=MESH
        )

    def send(src, dst, ssem, rsem, device, incoming=None):
        copy = remote(src, dst, ssem, rsem, device)
        copy.start()
        sends.append(copy)
        if incoming is not None:
            landing, sem = incoming
            copy = remote(landing, landing, ssem, sem, device)
        return copy

    chunks = [oc * 2, oc * 2 + 1, c * 2, c * 2 + 1]
    cols = [pl.ds(pl.multiple_of(g * 256, 256), 256) for g in chunks]
    load_w = pltpu.make_async_copy(w_hbm, w, load_s.at[0])
    load_pat = pltpu.make_async_copy(pat_hbm, pat, load_s.at[1])
    load_h = pltpu.make_async_copy(h_hbm, h, load_s.at[2])
    load_tf = [pltpu.make_async_copy(tf_hbm.at[:, cols[i]], tf.at[:, cols[i]], load_s.at[3 + i]) for i in range(4)]
    load_w.start()
    load_pat.start()
    for copy in load_tf:
        copy.start()
    load_h.start()

    barrier = pltpu.get_barrier_semaphore()
    greeted = [across] + [at_z(k) for k in (-2, 2)] + [at_xy(xy_of((2, 0)))]
    greeted += [at_xy(xy_of(off)) for off in ((1, 0), (3, 0), (0, 1))] + [at_z(k) for k in (-1, 1)] + [core]
    for device in greeted:
        pl.semaphore_signal(barrier, inc=1, device_id=device, device_id_type=MESH)

    load_w.wait()
    wt[...] = w[...].T
    gsend[...] = dot(wt[...], w[...], ((1,), (0,))).reshape(2, 128, K)
    load_pat.wait()

    def mask(i):
        load_tf[i].wait()
        for a in range(8):
            for b in range(2):
                rows = pl.ds(a * BLOCK, BLOCK)
                at = pl.ds(pl.multiple_of(chunks[i] * 256 + b * BLOCK, BLOCK), BLOCK)
                on = pat[a, chunks[i] * 2 + b].astype(F32).astype(BF16)
                masked[rows, at] = tf[rows, at] * on

    def numerator_h(i):
        return dot(wt[...], masked[:, cols[i]], ((1,), (0,)))

    mask(0)
    hsend[0] = numerator_h(0)
    pl.semaphore_wait(barrier, len(greeted))
    for device in (at_z(-2), at_z(2), at_xy(xy_of((0, 1)))):
        pl.semaphore_signal(ready1, inc=1, device_id=device, device_id_type=MESH)

    g_copy = send(gsend.at[oc], grecv, core_s.at[0], core_r.at[0], core)
    h_copy = [send(hsend.at[0], hrecv.at[0], core_s.at[1], core_r.at[1], core)]
    mask(1)
    hsend[1] = numerator_h(1)
    h_copy.append(send(hsend.at[1], hrecv.at[1], core_s.at[2], core_r.at[2], core))

    g_copy.wait_recv()
    part = gsend[c] + grecv[...]
    peak = jnp.max(part, axis=0, keepdims=True)
    gstep[...] = peak / LEVELS
    gcode[...] = encode(part, peak)
    gx = [
        send(gcode, gcode_in, x2_s.at[0], x2_r.at[0], across),
        send(gstep, gstep_in, x2_s.at[1], x2_r.at[1], across),
    ]
    hx = []
    for u in range(2):
        mask(2 + u)
        own = numerator_h(2 + u)
        h_copy[u].wait_recv()
        part = own + hrecv[u]
        peak = jnp.max(part, axis=0, keepdims=True)
        hstep[u] = peak / LEVELS
        hcode[u] = encode(part, peak)
        if u == 1:
            pl.semaphore_wait(ready1, 3)
            for k in (-4, 4):
                pl.semaphore_signal(ready2, inc=1, device_id=at_z(k), device_id_type=MESH)
        hx.append(send(hstep.at[u], hstep_in.at[u], x2_s.at[2 + u], x2_r.at[2 + u], across))
        hx.append(send(hcode.at[u], hcode_in.at[u], x2_s.at[4 + u], x2_r.at[4 + u], across))

    for copy in gx:
        copy.wait_recv()
    total = decode(gcode[...], gstep[...]) + decode(gcode_in[...], gstep_in[...])
    gram_w[c] = total.astype(BF16)
    gw = send(gram_w.at[c], gram_w.at[c], core_s.at[3], core_r.at[3], core)
    load_h.wait()
    gw.wait_recv()
    stores = []
    nh = []
    for u in range(2):
        hv = h[:, cols[2 + u]]
        den = dot(gram_w[...].reshape(K, K), hv, ((1,), (0,)))
        hx[2 * u].wait_recv()
        hx[2 * u + 1].wait_recv()
        total = decode(hcode[u], hstep[u]) + decode(hcode_in[u], hstep_in[u])
        new = (hv.astype(F32) * total / den).astype(BF16)
        g = chunks[2 + u]
        newh[g] = new
        theirs = newh.at[chunks[u]]
        nh.append(send(newh.at[g], newh.at[g], core_s.at[4 + u], core_r.at[4 + u], core, (theirs, core_r.at[4 + u])))
        stores.append(pltpu.make_async_copy(newh.at[g], outh.at[:, cols[2 + u]], store_s.at[u]))
        newht[pl.ds(pl.multiple_of(g * 256, 256), 256), :] = new.T

    rows = pl.ds(pl.multiple_of(xh * 128, 128), 128)
    for i in range(2):
        gpart[i] = sum(
            dot(newh[chunks[2 + u], rows, :], newht[pl.ds(pl.multiple_of(chunks[2 + u] * 256, 256), 256), i * 128 : i * 128 + 128], ((1,), (0,)))
            for u in range(2)
        )
    gxy = []
    n = 0
    for off in XY + ((0, 0),):
        p = xy_of(off)
        for dc in range(2):
            if off == (0, 0) and dc == 0:
                continue
            tc = lax.rem(c + dc, 2)
            tile = gpart.at[tc, pl.ds(pl.multiple_of(p * 16, 16), 16)]
            gxy.append(
                send(tile, gxy_in.at[n], gxy_s.at[n], gxy_r.at[n], {"doc": p * NZ + z, "term": xh * 2 + tc})
            )
            n += 1

    for u in range(2):
        g = chunks[u]
        nh[u].wait_recv()
        newht[pl.ds(pl.multiple_of(g * 256, 256), 256), :] = newh[g].T
        stores.append(pltpu.make_async_copy(newh.at[g], outh.at[:, cols[u]], store_s.at[2 + u]))

    for p in range(NXY):
        value = dot(masked[p * 128 : (p + 1) * 128, :], newht[...], ((1,), (0,)))
        acc[p] = value
        peak = jnp.max(value, axis=0, keepdims=True)
        code = encode(value, peak)
        step = peak / LEVELS
        for i in range(2):
            wstep[p, i] = step[:, i * 128 : (i + 1) * 128]
            for b in range(8):
                wcode[p, slot_at[i * 8 + b]] = code[b * 16 : (b + 1) * 16, i * 128 : (i + 1) * 128]
    wf, wn, ws = [], [], []
    for k, off in enumerate(XY):
        p = xy_of(off)
        ws.append(send(wstep.at[p], wstep_in.at[k], ws_s.at[k], ws_r.at[k], at_xy(p)))
        wf.append(send(wcode.at[p, NEAR:], wcode_in.at[k, NEAR:], wf_s.at[k], wf_r.at[k], at_xy(p)))
    for k, off in enumerate(XY):
        p = xy_of(off)
        wn.append(send(wcode.at[p, :NEAR], wcode_in.at[k, :NEAR], wn_s.at[k], wn_r.at[k], at_xy(p)))
    for copy in stores:
        copy.start()

    gsum = gpart[c, pl.ds(pl.multiple_of(q * 16, 16), 16), :]
    for n in range(15):
        gxy[n].wait_recv()
        gsum = gsum + gxy_in[n]
    gz[...] = gsum
    gz_in[z] = gsum
    pl.semaphore_wait(ready2, 2)
    gzc = []
    for k in ZS:
        p = z_at[k]
        gzc.append(send(gz, gz_in.at[z], gz_s.at[k], gz_r.at[z], at_z(k), (gz_in.at[p], gz_r.at[p])))

    def sum_xy(slots):
        for s in slots:
            half = half_at[s]
            total = acc[q, pl.ds(pl.multiple_of(row_at[s], 16), 16), pl.ds(pl.multiple_of(half * 128, 128), 128)]
            for k in range(7):
                total = total + decode(wcode_in[k, s], wstep_in[k, half])
            zsum[s] = total

    zs = {}
    for k in range(7):
        ws[k].wait_recv()
        wf[k].wait_recv()
    sum_xy(range(NEAR, NZ))
    for k in ZS[:7]:
        s = (k + 4) % NZ
        zs[s] = send(zsum.at[s], zsum_in.at[s], zs_s.at[s], zs_r.at[s], at_z(k))
    for k in range(7):
        wn[k].wait_recv()
    sum_xy(range(NEAR))
    for k in ZS[7:]:
        s = (k + 4) % NZ
        zs[s] = send(zsum.at[s], zsum_in.at[s], zs_s.at[s], zs_r.at[s], at_z(k))

    for copy in reversed(gzc):
        copy.wait_recv()
    gsum = gz_in[0]
    for p in range(1, NZ):
        gsum = gsum + gz_in[p]
    gfull[mine] = gsum.astype(BF16)
    gf = []
    n = 0
    for p_i, off in enumerate(XY + ((0, 0),)):
        p = xy_of(off)
        for dt in (2, 3, 1, 0):
            if off == (0, 0) and dt == 0:
                continue
            t = term_at[dt]
            at = gram_at[p_i, dt]
            device = {"doc": p * NZ + z, "term": t}
            gf.append(send(gfull.at[mine], gfull.at[mine], gf_s.at[n], gf_r.at[mine], device, (gfull.at[at], gf_r.at[at])))
            n += 1

    total = zsum[4]
    for s in range(NZ):
        if s != 4:
            zs[s].wait_recv()
            total = total + zsum_in[s]
    znum_in[4] = total
    zn = {}
    for k in ZS:
        s = (4 - k) % NZ
        zn[s] = send(znum_in.at[4], znum_in.at[s], zn_s.at[s], zn_r.at[s], at_z(k))

    for copy in reversed(gf):
        copy.wait_recv()
    for a in range(16):
        for i in range(2):
            gram_h[pl.ds(a * 16, 16), pl.ds(i * 128, 128)] = gfull[a * 2 + i]
    wrows = w[pl.ds(pl.multiple_of(q * 128, 128), 128), :]
    ratio[...] = wrows.astype(F32) / dot(wrows, gram_h[...], ((1,), (0,)))

    def spot(s):
        return pl.multiple_of(row_at[s], 16), pl.multiple_of(half_at[s] * 128, 128)

    def finish(slots):
        for s in slots:
            row, col = spot(s)
            tiles[q, s] = (ratio[pl.ds(row, 16), pl.ds(col, 128)] * znum_in[s]).astype(BF16)

    for s in range(NEAR):
        if s != 4:
            zn[s].wait_recv()
    finish(range(NEAR))
    on, of = [], []
    for k, off in enumerate(XY):
        src = tiles.at[q, :NEAR]
        p = xy_of(off)
        on.append(send(src, src, on_s.at[k], on_r.at[q], at_xy(p), (tiles.at[p, :NEAR], on_r.at[p])))
    for s in range(NEAR, NZ):
        zn[s].wait_recv()
    finish(range(NEAR, NZ))
    for k, off in enumerate(XY):
        src = tiles.at[q, NEAR:]
        p = xy_of(off)
        of.append(send(src, src, of_s.at[k], of_r.at[q], at_xy(p), (tiles.at[p, NEAR:], of_r.at[p])))

    def place(p, slots):
        for s in slots:
            row, col = spot(s)
            outw[pl.ds(pl.multiple_of(p * 128 + row, 16), 16), pl.ds(col, 128)] = tiles[p, s]

    place(q, range(NZ))
    for k, off in enumerate(XY):
        p = xy_of(off)
        on[k].wait_recv()
        place(p, range(NEAR))
    for k, off in enumerate(XY):
        p = xy_of(off)
        of[k].wait_recv()
        place(p, range(NEAR, NZ))
    for copy in sends:
        copy.wait_send()
    for copy in stores:
        copy.wait()


def on_device(tfidf, pattern, factor_w, factor_h):
    V = pltpu.VMEM
    scratch = [
        V((1024, 1024), BF16), V((1024, 1024), BF16), pltpu.SMEM((8, 8), jnp.int32),
        V((1024, K), BF16), V((K, 1024), BF16), V((K, 1024), BF16), V((4, K, 256), BF16), V((1024, K), BF16),
        V((2, K, 256), F32), V((2, K, 256), F32), V((2, K, 256), I16), V((2, K, 256), I16),
        V((2, 1, 256), F32), V((2, 1, 256), F32),
        V((2, 128, K), F32), V((128, K), F32), V((128, K), I16), V((128, K), I16), V((1, K), F32), V((1, K), F32),
        V((2, 128, K), BF16),
        V((2, 128, 128), F32), V((15, 16, 128), F32), V((16, 128), F32), V((NZ, 16, 128), F32),
        V((32, 16, 128), BF16), V((K, K), BF16), V((128, K), F32),
        V((NXY, NZ, 16, 128), I16), V((7, NZ, 16, 128), I16), V((NXY, 2, 1, 128), F32), V((7, 2, 1, 128), F32),
        V((NXY, 128, K), F32), V((NZ, 16, 128), F32), V((NZ, 16, 128), F32), V((NZ, 16, 128), F32),
        V((NXY, NZ, 16, 128), BF16),
    ]
    D = pltpu.SemaphoreType.DMA
    sems = [pltpu.SemaphoreType.REGULAR, pltpu.SemaphoreType.REGULAR, D((7,)), D((4,))]
    for a, b in ((6, 6), (6, 6), (15, 15), (NZ, NZ), (31, 32), (7, 7), (7, 7), (7, 7), (NZ, NZ), (NZ, NZ), (7, 8), (7, 8)):
        sems += [D((a,)), D((b,))]
    hbm = pl.BlockSpec(memory_space=pltpu.HBM)
    updated = pl.pallas_call(
        kernel,
        out_shape=(jax.ShapeDtypeStruct((1024, K), BF16), jax.ShapeDtypeStruct((K, 1024), BF16)),
        in_specs=[hbm] * 4,
        out_specs=(pl.BlockSpec(memory_space=pltpu.VMEM), pl.BlockSpec(memory_space=pl.ANY)),
        scratch_shapes=scratch + sems,
        compiler_params=pltpu.CompilerParams(
            collective_id=0, has_side_effects=True, vmem_limit_bytes=32 * 1024 * 1024
        ),
    )(*(pltpu.with_memory_space_constraint(a, pltpu.HBM) for a in (tfidf, pattern, factor_w, factor_h)))
    return pl.pallas_call(
        write_out,
        out_shape=(jax.ShapeDtypeStruct((1024, K), BF16), jax.ShapeDtypeStruct((K, 1024), BF16)),
        in_specs=[pl.BlockSpec(memory_space=pl.ANY)] * 2,
        out_specs=(pl.BlockSpec(memory_space=pl.ANY),) * 2,
        scratch_shapes=[D((2,))],
    )(*(pltpu.with_memory_space_constraint(a, pltpu.VMEM) for a in updated))


def write_out(w, h, outw, outh, sem):
    copies = [pltpu.make_async_copy(w, outw, sem.at[0]), pltpu.make_async_copy(h, outh, sem.at[1])]
    for copy in copies:
        copy.start()
    for copy in copies:
        copy.wait()


def solution(mesh):
    placed = (P("term", "doc"), P("term", "doc"), P("term", None), P(None, "doc"))
    return jax.shard_map(
        on_device,
        mesh=mesh,
        in_specs=placed,
        out_specs=(P("term", None), P(None, "doc")),
        check_vma=False,
    )
```

```python
import jax
import jax.numpy as jnp
from jax import lax
from jax.experimental import pallas as pl
from jax.experimental.pallas import tpu as pltpu
from jax.sharding import PartitionSpec as P

K = 256
BLOCK = 128
NXY = 8
NZ = 16
MESH = pl.DeviceIdType.MESH
F32 = jnp.float32
BF16 = jnp.bfloat16
I16 = jnp.int16
LEVELS = 65535.0
XY = ((2, 1), (2, 0), (1, 1), (3, 1), (1, 0), (3, 0), (0, 1))
ZS = (8, 7, 9, 6, 10, 5, 11, 4, 12, 3, 13, 2, 14, 1, 15)
NEAR = 9


def dot(a, b, dims):
    return lax.dot_general(a, b, (dims, ((), ())), preferred_element_type=F32)


def encode(value, peak):
    inv = jnp.where(peak > 0.0, LEVELS / peak, 0.0)
    return ((value * inv + 0.5).astype(jnp.int32) - 32768).astype(I16)


def decode(code, step):
    return (code.astype(jnp.int32) + 32768).astype(F32) * step


def kernel(
    tf_hbm, pat_hbm, w_hbm, h_hbm, outw, outh,
    tf, masked, pat, w, wt, h, newh, newht,
    hsend, hrecv, hcode, hcode_in, hstep, hstep_in,
    gsend, grecv, gcode, gcode_in, gstep, gstep_in, gram_w,
    gpart, gxy_in, gz, gz_in, gfull, gram_h, ratio,
    wcode, wcode_in, wstep, wstep_in, acc, zsum, zsum_in, znum_in, tiles,
    gz_step, gz_step_in, zown, zstep, zstep_in, znum_step,
    ready1, ready2,
    load_s, store_s, core_s, core_r, x2_s, x2_r, gxy_s, gxy_r, gz_s, gz_r, gf_s, gf_r,
    wf_s, wf_r, wn_s, wn_r, ws_s, ws_r, zs_s, zs_r, zn_s, zn_r, on_s, on_r, of_s, of_r,
    gt_s, gt_r, zt_s, zt_r, zm_s, zm_r,
):
    doc = lax.axis_index("doc")
    term = lax.axis_index("term")
    z = lax.rem(doc, NZ)
    q = lax.div(doc, NZ)
    y, xl = lax.div(q, 2), lax.rem(q, 2)
    xh = lax.div(term, 2)
    c = lax.rem(term, 2)
    oc = 1 - c

    def at_term(t):
        return {"doc": doc, "term": t}

    y_at = [lax.rem(y + i, 4) * 2 for i in range(4)]
    x_at = [xl, 1 - xl]
    xy_at = {off: y_at[off[0]] + x_at[off[1]] for off in ((0, 0),) + XY}
    z_at = [z] + [lax.rem(z + k, NZ) for k in range(1, NZ)]
    tile_at = [lax.rem(z + s + 12, NZ) for s in range(NZ)]
    half_at = [lax.div(tile, 8) for tile in tile_at]
    row_at = [lax.rem(tile, 8) * 16 for tile in tile_at]
    slot_at = [lax.rem(tile + 20 - z, NZ) for tile in range(NZ)]

    def xy_of(off):
        return xy_at[off]

    def at_xy(p):
        return {"doc": p * NZ + z, "term": term}

    def at_z(k):
        return {"doc": q * NZ + z_at[k % NZ], "term": term}

    term_at = [term] + [lax.rem(term + k, 4) for k in range(1, 4)]
    spread_at = [lax.div(t, 2) * (2 * NXY) + lax.rem(t, 2) for t in term_at]
    gram_at = {(i, dt): xy_at[off] * 2 + spread_at[dt] for i, off in enumerate(XY + ((0, 0),)) for dt in range(4)}
    mine = gram_at[len(XY), 0]

    core = at_term(xh * 2 + oc)
    across = at_term((1 - xh) * 2 + c)
    sends = []

    def remote(src, dst, ssem, rsem, device):
        return pltpu.make_async_remote_copy(
            src_ref=src, dst_ref=dst, send_sem=ssem, recv_sem=rsem, device_id=device, device_id_type=MESH
        )

    def send(src, dst, ssem, rsem, device, incoming=None):
        copy = remote(src, dst, ssem, rsem, device)
        copy.start()
        sends.append(copy)
        if incoming is not None:
            landing, sem = incoming
            copy = remote(landing, landing, ssem, sem, device)
        return copy

    chunks = [oc * 2, oc * 2 + 1, c * 2, c * 2 + 1]
    cols = [pl.ds(pl.multiple_of(g * 256, 256), 256) for g in chunks]
    load_w = pltpu.make_async_copy(w_hbm, w, load_s.at[0])
    load_pat = pltpu.make_async_copy(pat_hbm, pat, load_s.at[1])
    load_h = pltpu.make_async_copy(h_hbm, h, load_s.at[2])
    load_tf = [pltpu.make_async_copy(tf_hbm.at[:, cols[i]], tf.at[:, cols[i]], load_s.at[3 + i]) for i in range(4)]
    load_w.start()
    load_pat.start()
    for copy in load_tf:
        copy.start()
    load_h.start()

    barrier = pltpu.get_barrier_semaphore()
    greeted = [across] + [at_z(k) for k in (-2, 2)] + [at_xy(xy_of((2, 0)))]
    greeted += [at_xy(xy_of(off)) for off in ((1, 0), (3, 0), (0, 1))] + [at_z(k) for k in (-1, 1)] + [core]
    for device in greeted:
        pl.semaphore_signal(barrier, inc=1, device_id=device, device_id_type=MESH)

    load_w.wait()
    wt[...] = w[...].T
    gsend[...] = dot(wt[...], w[...], ((1,), (0,))).reshape(2, 128, K)
    def mask(i):
        load_tf[i].wait()
        for a in range(8):
            for b in range(2):
                rows = pl.ds(a * BLOCK, BLOCK)
                at = pl.ds(pl.multiple_of(chunks[i] * 256 + b * BLOCK, BLOCK), BLOCK)
                on = pat[a, chunks[i] * 2 + b].astype(F32).astype(BF16)
                masked[rows, at] = tf[rows, at] * on

    def numerator_h(i):
        return dot(wt[...], masked[:, cols[i]], ((1,), (0,)))

    pl.semaphore_wait(barrier, len(greeted))
    for device in (at_z(-2), at_z(2), at_xy(xy_of((0, 1)))):
        pl.semaphore_signal(ready1, inc=1, device_id=device, device_id_type=MESH)

    g_copy = send(gsend.at[oc], grecv, core_s.at[0], core_r.at[0], core)
    load_pat.wait()
    mask(0)
    hsend[0] = numerator_h(0)
    h_copy = [send(hsend.at[0], hrecv.at[0], core_s.at[1], core_r.at[1], core)]
    mask(1)
    hsend[1] = numerator_h(1)
    h_copy.append(send(hsend.at[1], hrecv.at[1], core_s.at[2], core_r.at[2], core))

    g_copy.wait_recv()
    part = gsend[c] + grecv[...]
    peak = jnp.max(part, axis=0, keepdims=True)
    gstep[...] = peak / LEVELS
    gcode[...] = encode(part, peak)
    gx = [
        send(gcode, gcode_in, x2_s.at[0], x2_r.at[0], across),
        send(gstep, gstep_in, x2_s.at[1], x2_r.at[1], across),
    ]
    hx = []
    for u in range(2):
        mask(2 + u)
        own = numerator_h(2 + u)
        h_copy[u].wait_recv()
        part = own + hrecv[u]
        peak = jnp.max(part, axis=0, keepdims=True)
        hstep[u] = peak / LEVELS
        hcode[u] = encode(part, peak)
        if u == 1:
            pl.semaphore_wait(ready1, 3)
            for k in (-4, 4):
                pl.semaphore_signal(ready2, inc=1, device_id=at_z(k), device_id_type=MESH)
        hx.append(send(hstep.at[u], hstep_in.at[u], x2_s.at[2 + u], x2_r.at[2 + u], across))
        hx.append(send(hcode.at[u], hcode_in.at[u], x2_s.at[4 + u], x2_r.at[4 + u], across))

    for copy in gx:
        copy.wait_recv()
    total = decode(gcode[...], gstep[...]) + decode(gcode_in[...], gstep_in[...])
    gram_w[c] = total.astype(BF16)
    gw = send(gram_w.at[c], gram_w.at[c], core_s.at[3], core_r.at[3], core)
    load_h.wait()
    gw.wait_recv()
    stores = []
    nh = []
    for u in range(2):
        hv = h[:, cols[2 + u]]
        den = dot(gram_w[...].reshape(K, K), hv, ((1,), (0,)))
        hx[2 * u].wait_recv()
        hx[2 * u + 1].wait_recv()
        total = decode(hcode[u], hstep[u]) + decode(hcode_in[u], hstep_in[u])
        new = (hv.astype(F32) * total / den).astype(BF16)
        g = chunks[2 + u]
        newh[g] = new
        theirs = newh.at[chunks[u]]
        nh.append(send(newh.at[g], newh.at[g], core_s.at[4 + u], core_r.at[4 + u], core, (theirs, core_r.at[4 + u])))
        stores.append(pltpu.make_async_copy(newh.at[g], outh.at[:, cols[2 + u]], store_s.at[u]))
        newht[pl.ds(pl.multiple_of(g * 256, 256), 256), :] = new.T

    rows = pl.ds(pl.multiple_of(xh * 128, 128), 128)
    for i in range(2):
        gpart[i] = sum(
            dot(newh[chunks[2 + u], rows, :], newht[pl.ds(pl.multiple_of(chunks[2 + u] * 256, 256), 256), i * 128 : i * 128 + 128], ((1,), (0,)))
            for u in range(2)
        )
    gxy = []
    n = 0
    for off in XY + ((0, 0),):
        p = xy_of(off)
        for dc in range(2):
            if off == (0, 0) and dc == 0:
                continue
            tc = lax.rem(c + dc, 2)
            tile = gpart.at[tc, pl.ds(pl.multiple_of(p * 16, 16), 16)]
            gxy.append(
                send(tile, gxy_in.at[n], gxy_s.at[n], gxy_r.at[n], {"doc": p * NZ + z, "term": xh * 2 + tc})
            )
            n += 1

    for u in range(2):
        g = chunks[u]
        nh[u].wait_recv()
        newht[pl.ds(pl.multiple_of(g * 256, 256), 256), :] = newh[g].T
        stores.append(pltpu.make_async_copy(newh.at[g], outh.at[:, cols[u]], store_s.at[2 + u]))

    for p in range(NXY):
        value = dot(masked[p * 128 : (p + 1) * 128, :], newht[...], ((1,), (0,)))
        acc[p] = value
        peak = jnp.max(value, axis=0, keepdims=True)
        code = encode(value, peak)
        step = peak / LEVELS
        for i in range(2):
            wstep[p, i] = step[:, i * 128 : (i + 1) * 128]
            for b in range(8):
                wcode[p, slot_at[i * 8 + b]] = code[b * 16 : (b + 1) * 16, i * 128 : (i + 1) * 128]
    wf, wn, ws = [], [], []
    for k, off in enumerate(XY):
        p = xy_of(off)
        ws.append(send(wstep.at[p], wstep_in.at[k], ws_s.at[k], ws_r.at[k], at_xy(p)))
        wf.append(send(wcode.at[p, NEAR:], wcode_in.at[k, NEAR:], wf_s.at[k], wf_r.at[k], at_xy(p)))
    for k, off in enumerate(XY):
        p = xy_of(off)
        wn.append(send(wcode.at[p, :NEAR], wcode_in.at[k, :NEAR], wn_s.at[k], wn_r.at[k], at_xy(p)))
    for copy in stores:
        copy.start()

    gsum = gpart[c, pl.ds(pl.multiple_of(q * 16, 16), 16), :]
    for n in range(15):
        gxy[n].wait_recv()
        gsum = gsum + gxy_in[n]
    peak = jnp.max(gsum, axis=0, keepdims=True)
    gz_step[...] = peak / LEVELS
    gz_step_in[z] = peak / LEVELS
    code = encode(gsum, peak)
    gz[...] = code
    gz_in[z] = code
    pl.semaphore_wait(ready2, 2)
    gzc = []
    for k in ZS:
        p = z_at[k]
        gzc.append(send(gz_step, gz_step_in.at[z], gt_s.at[k], gt_r.at[z], at_z(k), (gz_step_in.at[p], gt_r.at[p])))
        gzc.append(send(gz, gz_in.at[z], gz_s.at[k], gz_r.at[z], at_z(k), (gz_in.at[p], gz_r.at[p])))

    def sum_xy(slots):
        for s in slots:
            half = half_at[s]
            total = acc[q, pl.ds(pl.multiple_of(row_at[s], 16), 16), pl.ds(pl.multiple_of(half * 128, 128), 128)]
            for k in range(7):
                total = total + decode(wcode_in[k, s], wstep_in[k, half])
            if s == 4:
                zown[...] = total
                continue
            peak = jnp.max(total, axis=0, keepdims=True)
            zstep[s] = peak / LEVELS
            zsum[s] = encode(total, peak)

    zs, zt = {}, {}
    for k in range(7):
        ws[k].wait_recv()
        wf[k].wait_recv()
    sum_xy(range(NEAR, NZ))
    for k in ZS[:7]:
        s = (k + 4) % NZ
        zt[s] = send(zstep.at[s], zstep_in.at[s], zt_s.at[s], zt_r.at[s], at_z(k))
        zs[s] = send(zsum.at[s], zsum_in.at[s], zs_s.at[s], zs_r.at[s], at_z(k))
    for k in range(7):
        wn[k].wait_recv()
    sum_xy(range(NEAR))
    for k in ZS[7:]:
        s = (k + 4) % NZ
        zt[s] = send(zstep.at[s], zstep_in.at[s], zt_s.at[s], zt_r.at[s], at_z(k))
        zs[s] = send(zsum.at[s], zsum_in.at[s], zs_s.at[s], zs_r.at[s], at_z(k))

    for copy in reversed(gzc):
        copy.wait_recv()
    gsum = decode(gz_in[0], gz_step_in[0])
    for p in range(1, NZ):
        gsum = gsum + decode(gz_in[p], gz_step_in[p])
    gfull[mine] = gsum.astype(BF16)
    gf = []
    n = 0
    for p_i, off in enumerate(XY + ((0, 0),)):
        p = xy_of(off)
        for dt in (2, 3, 1, 0):
            if off == (0, 0) and dt == 0:
                continue
            t = term_at[dt]
            at = gram_at[p_i, dt]
            device = {"doc": p * NZ + z, "term": t}
            gf.append(send(gfull.at[mine], gfull.at[mine], gf_s.at[n], gf_r.at[mine], device, (gfull.at[at], gf_r.at[at])))
            n += 1

    total = zown[...]
    for s in range(NZ):
        if s != 4:
            zt[s].wait_recv()
            zs[s].wait_recv()
            total = total + decode(zsum_in[s], zstep_in[s])
    peak = jnp.max(total, axis=0, keepdims=True)
    znum_in[4] = encode(total, peak)
    znum_step[4] = peak / LEVELS
    zn, zm = {}, {}
    for k in ZS:
        s = (4 - k) % NZ
        zm[s] = send(znum_step.at[4], znum_step.at[s], zm_s.at[s], zm_r.at[s], at_z(k))
        zn[s] = send(znum_in.at[4], znum_in.at[s], zn_s.at[s], zn_r.at[s], at_z(k))

    for copy in reversed(gf):
        copy.wait_recv()
    for a in range(16):
        for i in range(2):
            gram_h[pl.ds(a * 16, 16), pl.ds(i * 128, 128)] = gfull[a * 2 + i]
    wrows = w[pl.ds(pl.multiple_of(q * 128, 128), 128), :]
    ratio[...] = wrows.astype(F32) / dot(wrows, gram_h[...], ((1,), (0,)))

    def spot(s):
        return pl.multiple_of(row_at[s], 16), pl.multiple_of(half_at[s] * 128, 128)

    def finish(slots):
        for s in slots:
            row, col = spot(s)
            tiles[q, s] = (ratio[pl.ds(row, 16), pl.ds(col, 128)] * decode(znum_in[s], znum_step[s])).astype(BF16)

    for s in range(NEAR):
        if s != 4:
            zm[s].wait_recv()
            zn[s].wait_recv()
    finish(range(NEAR))
    on, of = [], []
    for k, off in enumerate(XY):
        src = tiles.at[q, :NEAR]
        p = xy_of(off)
        on.append(send(src, src, on_s.at[k], on_r.at[q], at_xy(p), (tiles.at[p, :NEAR], on_r.at[p])))
    for s in range(NEAR, NZ):
        zm[s].wait_recv()
        zn[s].wait_recv()
    finish(range(NEAR, NZ))
    for k, off in enumerate(XY):
        src = tiles.at[q, NEAR:]
        p = xy_of(off)
        of.append(send(src, src, of_s.at[k], of_r.at[q], at_xy(p), (tiles.at[p, NEAR:], of_r.at[p])))

    def place(p, slots):
        for s in slots:
            row, col = spot(s)
            outw[pl.ds(pl.multiple_of(p * 128 + row, 16), 16), pl.ds(col, 128)] = tiles[p, s]

    place(q, range(NZ))
    for k, off in enumerate(XY):
        p = xy_of(off)
        on[k].wait_recv()
        place(p, range(NEAR))
    for k, off in enumerate(XY):
        p = xy_of(off)
        of[k].wait_recv()
        place(p, range(NEAR, NZ))
    for copy in sends:
        copy.wait_send()
    for copy in stores:
        copy.wait()


def on_device(tfidf, pattern, factor_w, factor_h):
    V = pltpu.VMEM
    scratch = [
        V((1024, 1024), BF16), V((1024, 1024), BF16), pltpu.SMEM((8, 8), jnp.int32),
        V((1024, K), BF16), V((K, 1024), BF16), V((K, 1024), BF16), V((4, K, 256), BF16), V((1024, K), BF16),
        V((2, K, 256), F32), V((2, K, 256), F32), V((2, K, 256), I16), V((2, K, 256), I16),
        V((2, 1, 256), F32), V((2, 1, 256), F32),
        V((2, 128, K), F32), V((128, K), F32), V((128, K), I16), V((128, K), I16), V((1, K), F32), V((1, K), F32),
        V((2, 128, K), BF16),
        V((2, 128, 128), F32), V((15, 16, 128), F32), V((16, 128), I16), V((NZ, 16, 128), I16),
        V((32, 16, 128), BF16), V((K, K), BF16), V((128, K), F32),
        V((NXY, NZ, 16, 128), I16), V((7, NZ, 16, 128), I16), V((NXY, 2, 1, 128), F32), V((7, 2, 1, 128), F32),
        V((NXY, 128, K), F32), V((NZ, 16, 128), I16), V((NZ, 16, 128), I16), V((NZ, 16, 128), I16),
        V((NXY, NZ, 16, 128), BF16),
        V((1, 128), F32), V((NZ, 1, 128), F32), V((16, 128), F32), V((NZ, 1, 128), F32), V((NZ, 1, 128), F32), V((NZ, 1, 128), F32),
    ]
    D = pltpu.SemaphoreType.DMA
    sems = [pltpu.SemaphoreType.REGULAR, pltpu.SemaphoreType.REGULAR, D((7,)), D((4,))]
    for a, b in ((6, 6), (6, 6), (15, 15), (NZ, NZ), (31, 32), (7, 7), (7, 7), (7, 7), (NZ, NZ), (NZ, NZ), (7, 8), (7, 8), (NZ, NZ), (NZ, NZ), (NZ, NZ)):
        sems += [D((a,)), D((b,))]
    hbm = pl.BlockSpec(memory_space=pltpu.HBM)
    updated = pl.pallas_call(
        kernel,
        out_shape=(jax.ShapeDtypeStruct((1024, K), BF16), jax.ShapeDtypeStruct((K, 1024), BF16)),
        in_specs=[hbm] * 4,
        out_specs=(pl.BlockSpec(memory_space=pltpu.VMEM), pl.BlockSpec(memory_space=pl.ANY)),
        scratch_shapes=scratch + sems,
        compiler_params=pltpu.CompilerParams(
            collective_id=0, has_side_effects=True, vmem_limit_bytes=32 * 1024 * 1024
        ),
    )(*(pltpu.with_memory_space_constraint(a, pltpu.HBM) for a in (tfidf, pattern, factor_w, factor_h)))
    return pl.pallas_call(
        write_out,
        out_shape=(jax.ShapeDtypeStruct((1024, K), BF16), jax.ShapeDtypeStruct((K, 1024), BF16)),
        in_specs=[pl.BlockSpec(memory_space=pl.ANY)] * 2,
        out_specs=(pl.BlockSpec(memory_space=pl.ANY),) * 2,
        scratch_shapes=[D((2,))],
    )(*(pltpu.with_memory_space_constraint(a, pltpu.VMEM) for a in updated))


def write_out(w, h, outw, outh, sem):
    copies = [pltpu.make_async_copy(w, outw, sem.at[0]), pltpu.make_async_copy(h, outh, sem.at[1])]
    for copy in copies:
        copy.start()
    for copy in copies:
        copy.wait()


def solution(mesh):
    placed = (P("term", "doc"), P("term", "doc"), P("term", None), P(None, "doc"))
    return jax.shard_map(
        on_device,
        mesh=mesh,
        in_specs=placed,
        out_specs=(P("term", None), P(None, "doc")),
        check_vma=False,
    )
```

```python
import jax
import jax.numpy as jnp
from jax import lax
from jax.experimental import pallas as pl
from jax.experimental.pallas import tpu as pltpu
from jax.sharding import PartitionSpec as P

K = 256
BLOCK = 128
NXY = 8
NZ = 16
MESH = pl.DeviceIdType.MESH
F32 = jnp.float32
BF16 = jnp.bfloat16
I16 = jnp.int16
LEVELS = 65535.0
XY = ((2, 1), (2, 0), (1, 1), (3, 1), (1, 0), (3, 0), (0, 1))
ZS = (8, 7, 9, 6, 10, 5, 11, 4, 12, 3, 13, 2, 14, 1, 15)
NEAR = 9


def dot(a, b, dims):
    return lax.dot_general(a, b, (dims, ((), ())), preferred_element_type=F32)


def encode(value, peak):
    inv = jnp.where(peak > 0.0, LEVELS / peak, 0.0)
    return ((value * inv + 0.5).astype(jnp.int32) - 32768).astype(I16)


def decode(code, step):
    return (code.astype(jnp.int32) + 32768).astype(F32) * step


def kernel(
    tf_hbm, pat_hbm, w_hbm, h_hbm, outw, outh,
    tf, masked, pat, w, wt, h, newh, newht,
    hsend, hrecv, hcode, hcode_in, hstep, hstep_in,
    gsend, grecv, gcode, gcode_in, gstep, gstep_in, gram_w,
    gpart, gxy_in, gz, gz_in, gfull, gram_h, ratio,
    wcode, wcode_in, wstep, wstep_in, acc, zsum, zsum_in, znum_in, tiles,
    gz_step, gz_step_in, zown, zstep, zstep_in, znum_step,
    ready1, ready2,
    load_s, store_s, core_s, core_r, x2_s, x2_r, gxy_s, gxy_r, gz_s, gz_r, gf_s, gf_r,
    wf_s, wf_r, wn_s, wn_r, ws_s, ws_r, zs_s, zs_r, zn_s, zn_r, on_s, on_r, of_s, of_r,
    gt_s, gt_r, zt_s, zt_r, zm_s, zm_r,
):
    doc = lax.axis_index("doc")
    term = lax.axis_index("term")
    z = lax.rem(doc, NZ)
    q = lax.div(doc, NZ)
    y, xl = lax.div(q, 2), lax.rem(q, 2)
    xh = lax.div(term, 2)
    c = lax.rem(term, 2)
    oc = 1 - c

    def at_term(t):
        return {"doc": doc, "term": t}

    y_at = [lax.rem(y + i, 4) * 2 for i in range(4)]
    x_at = [xl, 1 - xl]
    xy_at = {off: y_at[off[0]] + x_at[off[1]] for off in ((0, 0),) + XY}
    z_at = [z] + [lax.rem(z + k, NZ) for k in range(1, NZ)]
    tile_at = [lax.rem(z + s + 12, NZ) for s in range(NZ)]
    half_at = [lax.div(tile, 8) for tile in tile_at]
    row_at = [lax.rem(tile, 8) * 16 for tile in tile_at]
    slot_at = [lax.rem(tile + 20 - z, NZ) for tile in range(NZ)]

    def xy_of(off):
        return xy_at[off]

    def at_xy(p):
        return {"doc": p * NZ + z, "term": term}

    def at_z(k):
        return {"doc": q * NZ + z_at[k % NZ], "term": term}

    term_at = [term] + [lax.rem(term + k, 4) for k in range(1, 4)]
    spread_at = [lax.div(t, 2) * (2 * NXY) + lax.rem(t, 2) for t in term_at]
    gram_at = {(i, dt): xy_at[off] * 2 + spread_at[dt] for i, off in enumerate(XY + ((0, 0),)) for dt in range(4)}
    mine = gram_at[len(XY), 0]

    core = at_term(xh * 2 + oc)
    across = at_term((1 - xh) * 2 + c)
    sends = []

    def remote(src, dst, ssem, rsem, device):
        return pltpu.make_async_remote_copy(
            src_ref=src, dst_ref=dst, send_sem=ssem, recv_sem=rsem, device_id=device, device_id_type=MESH
        )

    def send(src, dst, ssem, rsem, device, incoming=None):
        copy = remote(src, dst, ssem, rsem, device)
        copy.start()
        sends.append(copy)
        if incoming is not None:
            landing, sem = incoming
            copy = remote(landing, landing, ssem, sem, device)
        return copy

    chunks = [oc * 2, oc * 2 + 1, c * 2, c * 2 + 1]
    cols = [pl.ds(pl.multiple_of(g * 256, 256), 256) for g in chunks]
    load_w = pltpu.make_async_copy(w_hbm, w, load_s.at[0])
    load_pat = pltpu.make_async_copy(pat_hbm, pat, load_s.at[1])
    load_h = pltpu.make_async_copy(h_hbm, h, load_s.at[2])
    load_tf = [pltpu.make_async_copy(tf_hbm.at[:, cols[i]], tf.at[:, cols[i]], load_s.at[3 + i]) for i in range(4)]
    load_w.start()
    load_pat.start()
    for copy in load_tf:
        copy.start()
    load_h.start()

    barrier = pltpu.get_barrier_semaphore()
    greeted = [across] + [at_z(k) for k in (-2, 2)] + [at_xy(xy_of((2, 0)))]
    greeted += [at_xy(xy_of(off)) for off in ((1, 0), (3, 0), (0, 1))] + [at_z(k) for k in (-1, 1)] + [core]
    for device in greeted:
        pl.semaphore_signal(barrier, inc=1, device_id=device, device_id_type=MESH)

    load_w.wait()
    wt[...] = w[...].T
    gsend[...] = dot(wt[...], w[...], ((1,), (0,))).reshape(2, 128, K)
    def mask(i):
        load_tf[i].wait()
        for a in range(8):
            for b in range(2):
                rows = pl.ds(a * BLOCK, BLOCK)
                at = pl.ds(pl.multiple_of(chunks[i] * 256 + b * BLOCK, BLOCK), BLOCK)
                on = pat[a, chunks[i] * 2 + b].astype(F32).astype(BF16)
                masked[rows, at] = tf[rows, at] * on

    def numerator_h(i):
        return dot(wt[...], masked[:, cols[i]], ((1,), (0,)))

    pl.semaphore_wait(barrier, len(greeted))
    for device in (at_z(-2), at_z(2), at_xy(xy_of((0, 1)))):
        pl.semaphore_signal(ready1, inc=1, device_id=device, device_id_type=MESH)

    g_copy = send(gsend.at[oc], grecv, core_s.at[0], core_r.at[0], core)
    load_pat.wait()
    mask(0)
    hsend[0] = numerator_h(0)
    h_copy = [send(hsend.at[0], hrecv.at[0], core_s.at[1], core_r.at[1], core)]
    mask(1)
    hsend[1] = numerator_h(1)
    h_copy.append(send(hsend.at[1], hrecv.at[1], core_s.at[2], core_r.at[2], core))

    g_copy.wait_recv()
    part = gsend[c] + grecv[...]
    peak = jnp.max(part, axis=0, keepdims=True)
    gstep[...] = peak / LEVELS
    gcode[...] = encode(part, peak)
    gx = [
        send(gcode, gcode_in, x2_s.at[0], x2_r.at[0], across),
        send(gstep, gstep_in, x2_s.at[1], x2_r.at[1], across),
    ]
    hx = []
    for u in range(2):
        mask(2 + u)
        own = numerator_h(2 + u)
        h_copy[u].wait_recv()
        part = own + hrecv[u]
        peak = jnp.max(part, axis=0, keepdims=True)
        hstep[u] = peak / LEVELS
        hcode[u] = encode(part, peak)
        if u == 1:
            pl.semaphore_wait(ready1, 3)
            for k in (-4, 4):
                pl.semaphore_signal(ready2, inc=1, device_id=at_z(k), device_id_type=MESH)
        hx.append(send(hstep.at[u], hstep_in.at[u], x2_s.at[2 + u], x2_r.at[2 + u], across))
        hx.append(send(hcode.at[u], hcode_in.at[u], x2_s.at[4 + u], x2_r.at[4 + u], across))

    for copy in gx:
        copy.wait_recv()
    total = decode(gcode[...], gstep[...]) + decode(gcode_in[...], gstep_in[...])
    gram_w[c] = total.astype(BF16)
    gw = send(gram_w.at[c], gram_w.at[c], core_s.at[3], core_r.at[3], core)
    load_h.wait()
    gw.wait_recv()
    stores = []
    nh = []
    for u in range(2):
        hv = h[:, cols[2 + u]]
        den = dot(gram_w[...].reshape(K, K), hv, ((1,), (0,)))
        hx[2 * u].wait_recv()
        hx[2 * u + 1].wait_recv()
        total = decode(hcode[u], hstep[u]) + decode(hcode_in[u], hstep_in[u])
        new = (hv.astype(F32) * total / den).astype(BF16)
        g = chunks[2 + u]
        newh[g] = new
        theirs = newh.at[chunks[u]]
        nh.append(send(newh.at[g], newh.at[g], core_s.at[4 + u], core_r.at[4 + u], core, (theirs, core_r.at[4 + u])))
        stores.append(pltpu.make_async_copy(newh.at[g], outh.at[:, cols[2 + u]], store_s.at[u]))
        newht[pl.ds(pl.multiple_of(g * 256, 256), 256), :] = new.T

    rows = pl.ds(pl.multiple_of(xh * 128, 128), 128)
    for i in range(2):
        gpart[i] = sum(
            dot(newh[chunks[2 + u], rows, :], newht[pl.ds(pl.multiple_of(chunks[2 + u] * 256, 256), 256), i * 128 : i * 128 + 128], ((1,), (0,)))
            for u in range(2)
        )
    gxy = []
    n = 0
    for off in XY + ((0, 0),):
        p = xy_of(off)
        for dc in range(2):
            if off == (0, 0) and dc == 0:
                continue
            tc = lax.rem(c + dc, 2)
            tile = gpart.at[tc, pl.ds(pl.multiple_of(p * 16, 16), 16)]
            gxy.append(
                send(tile, gxy_in.at[n], gxy_s.at[n], gxy_r.at[n], {"doc": p * NZ + z, "term": xh * 2 + tc})
            )
            n += 1

    half = pl.ds(pl.multiple_of(c * 512, 512), 512)
    for p in range(NXY):
        acc[p] = dot(masked[p * 128 : (p + 1) * 128, half], newht[half, :], ((1,), (0,)))

    for u in range(2):
        g = chunks[u]
        nh[u].wait_recv()
        newht[cols[u], :] = newh[g].T
        if u == 0:
            for p in range(NXY):
                acc[p] += dot(masked[p * 128 : (p + 1) * 128, cols[0]], newht[cols[0], :], ((1,), (0,)))
        stores.append(pltpu.make_async_copy(newh.at[g], outh.at[:, cols[u]], store_s.at[2 + u]))

    for p in range(NXY):
        value = acc[p] + dot(masked[p * 128 : (p + 1) * 128, cols[1]], newht[cols[1], :], ((1,), (0,)))
        acc[p] = value
        peak = jnp.max(value, axis=0, keepdims=True)
        code = encode(value, peak)
        step = peak / LEVELS
        for i in range(2):
            wstep[p, i] = step[:, i * 128 : (i + 1) * 128]
            for b in range(8):
                wcode[p, slot_at[i * 8 + b]] = code[b * 16 : (b + 1) * 16, i * 128 : (i + 1) * 128]
    wf, wn, ws = [], [], []
    for k, off in enumerate(XY):
        p = xy_of(off)
        ws.append(send(wstep.at[p], wstep_in.at[k], ws_s.at[k], ws_r.at[k], at_xy(p)))
        wf.append(send(wcode.at[p, NEAR:], wcode_in.at[k, NEAR:], wf_s.at[k], wf_r.at[k], at_xy(p)))
    for k, off in enumerate(XY):
        p = xy_of(off)
        wn.append(send(wcode.at[p, :NEAR], wcode_in.at[k, :NEAR], wn_s.at[k], wn_r.at[k], at_xy(p)))
    for copy in stores:
        copy.start()

    gsum = gpart[c, pl.ds(pl.multiple_of(q * 16, 16), 16), :]
    for n in range(15):
        gxy[n].wait_recv()
        gsum = gsum + gxy_in[n]
    peak = jnp.max(gsum, axis=0, keepdims=True)
    gz_step[...] = peak / LEVELS
    gz_step_in[z] = peak / LEVELS
    code = encode(gsum, peak)
    gz[...] = code
    gz_in[z] = code
    pl.semaphore_wait(ready2, 2)
    gzc = []
    for k in ZS:
        p = z_at[k]
        gzc.append(send(gz_step, gz_step_in.at[z], gt_s.at[k], gt_r.at[z], at_z(k), (gz_step_in.at[p], gt_r.at[p])))
        gzc.append(send(gz, gz_in.at[z], gz_s.at[k], gz_r.at[z], at_z(k), (gz_in.at[p], gz_r.at[p])))

    def sum_xy(slots):
        for s in slots:
            half = half_at[s]
            total = acc[q, pl.ds(pl.multiple_of(row_at[s], 16), 16), pl.ds(pl.multiple_of(half * 128, 128), 128)]
            for k in range(7):
                total = total + decode(wcode_in[k, s], wstep_in[k, half])
            if s == 4:
                zown[...] = total
                continue
            peak = jnp.max(total, axis=0, keepdims=True)
            zstep[s] = peak / LEVELS
            zsum[s] = encode(total, peak)

    zs, zt = {}, {}
    for k in range(7):
        ws[k].wait_recv()
        wf[k].wait_recv()
    sum_xy(range(NEAR, NZ))
    for k in ZS[:7]:
        s = (k + 4) % NZ
        zt[s] = send(zstep.at[s], zstep_in.at[s], zt_s.at[s], zt_r.at[s], at_z(k))
        zs[s] = send(zsum.at[s], zsum_in.at[s], zs_s.at[s], zs_r.at[s], at_z(k))
    for k in range(7):
        wn[k].wait_recv()
    sum_xy(range(NEAR))
    for k in ZS[7:]:
        s = (k + 4) % NZ
        zt[s] = send(zstep.at[s], zstep_in.at[s], zt_s.at[s], zt_r.at[s], at_z(k))
        zs[s] = send(zsum.at[s], zsum_in.at[s], zs_s.at[s], zs_r.at[s], at_z(k))

    for copy in reversed(gzc):
        copy.wait_recv()
    gsum = decode(gz_in[0], gz_step_in[0])
    for p in range(1, NZ):
        gsum = gsum + decode(gz_in[p], gz_step_in[p])
    gfull[mine] = gsum.astype(BF16)
    gf = []
    n = 0
    for p_i, off in enumerate(XY + ((0, 0),)):
        p = xy_of(off)
        for dt in (2, 3, 1, 0):
            if off == (0, 0) and dt == 0:
                continue
            t = term_at[dt]
            at = gram_at[p_i, dt]
            device = {"doc": p * NZ + z, "term": t}
            gf.append(send(gfull.at[mine], gfull.at[mine], gf_s.at[n], gf_r.at[mine], device, (gfull.at[at], gf_r.at[at])))
            n += 1

    total = zown[...]
    for s in range(NZ):
        if s != 4:
            zt[s].wait_recv()
            zs[s].wait_recv()
            total = total + decode(zsum_in[s], zstep_in[s])
    peak = jnp.max(total, axis=0, keepdims=True)
    znum_in[4] = encode(total, peak)
    znum_step[4] = peak / LEVELS
    zn, zm = {}, {}
    for k in ZS:
        s = (4 - k) % NZ
        zm[s] = send(znum_step.at[4], znum_step.at[s], zm_s.at[s], zm_r.at[s], at_z(k))
        zn[s] = send(znum_in.at[4], znum_in.at[s], zn_s.at[s], zn_r.at[s], at_z(k))

    for copy in reversed(gf):
        copy.wait_recv()
    for a in range(16):
        for i in range(2):
            gram_h[pl.ds(a * 16, 16), pl.ds(i * 128, 128)] = gfull[a * 2 + i]
    wrows = w[pl.ds(pl.multiple_of(q * 128, 128), 128), :]
    ratio[...] = wrows.astype(F32) / dot(wrows, gram_h[...], ((1,), (0,)))

    def spot(s):
        return pl.multiple_of(row_at[s], 16), pl.multiple_of(half_at[s] * 128, 128)

    def finish(slots):
        for s in slots:
            row, col = spot(s)
            tiles[q, s] = (ratio[pl.ds(row, 16), pl.ds(col, 128)] * decode(znum_in[s], znum_step[s])).astype(BF16)

    for s in range(NEAR):
        if s != 4:
            zm[s].wait_recv()
            zn[s].wait_recv()
    finish(range(NEAR))
    on, of = [], []
    for k, off in enumerate(XY):
        src = tiles.at[q, :NEAR]
        p = xy_of(off)
        on.append(send(src, src, on_s.at[k], on_r.at[q], at_xy(p), (tiles.at[p, :NEAR], on_r.at[p])))
    for s in range(NEAR, NZ):
        zm[s].wait_recv()
        zn[s].wait_recv()
    finish(range(NEAR, NZ))
    for k, off in enumerate(XY):
        src = tiles.at[q, NEAR:]
        p = xy_of(off)
        of.append(send(src, src, of_s.at[k], of_r.at[q], at_xy(p), (tiles.at[p, NEAR:], of_r.at[p])))

    def place(p, slots):
        for s in slots:
            row, col = spot(s)
            outw[pl.ds(pl.multiple_of(p * 128 + row, 16), 16), pl.ds(col, 128)] = tiles[p, s]

    place(q, range(NZ))
    for k, off in enumerate(XY):
        p = xy_of(off)
        on[k].wait_recv()
        place(p, range(NEAR))
    for k, off in enumerate(XY):
        p = xy_of(off)
        of[k].wait_recv()
        place(p, range(NEAR, NZ))
    for copy in sends:
        copy.wait_send()
    for copy in stores:
        copy.wait()


def on_device(tfidf, pattern, factor_w, factor_h):
    V = pltpu.VMEM
    scratch = [
        V((1024, 1024), BF16), V((1024, 1024), BF16), pltpu.SMEM((8, 8), jnp.int32),
        V((1024, K), BF16), V((K, 1024), BF16), V((K, 1024), BF16), V((4, K, 256), BF16), V((1024, K), BF16),
        V((2, K, 256), F32), V((2, K, 256), F32), V((2, K, 256), I16), V((2, K, 256), I16),
        V((2, 1, 256), F32), V((2, 1, 256), F32),
        V((2, 128, K), F32), V((128, K), F32), V((128, K), I16), V((128, K), I16), V((1, K), F32), V((1, K), F32),
        V((2, 128, K), BF16),
        V((2, 128, 128), F32), V((15, 16, 128), F32), V((16, 128), I16), V((NZ, 16, 128), I16),
        V((32, 16, 128), BF16), V((K, K), BF16), V((128, K), F32),
        V((NXY, NZ, 16, 128), I16), V((7, NZ, 16, 128), I16), V((NXY, 2, 1, 128), F32), V((7, 2, 1, 128), F32),
        V((NXY, 128, K), F32), V((NZ, 16, 128), I16), V((NZ, 16, 128), I16), V((NZ, 16, 128), I16),
        V((NXY, NZ, 16, 128), BF16),
        V((1, 128), F32), V((NZ, 1, 128), F32), V((16, 128), F32), V((NZ, 1, 128), F32), V((NZ, 1, 128), F32), V((NZ, 1, 128), F32),
    ]
    D = pltpu.SemaphoreType.DMA
    sems = [pltpu.SemaphoreType.REGULAR, pltpu.SemaphoreType.REGULAR, D((7,)), D((4,))]
    for a, b in ((6, 6), (6, 6), (15, 15), (NZ, NZ), (31, 32), (7, 7), (7, 7), (7, 7), (NZ, NZ), (NZ, NZ), (7, 8), (7, 8), (NZ, NZ), (NZ, NZ), (NZ, NZ)):
        sems += [D((a,)), D((b,))]
    hbm = pl.BlockSpec(memory_space=pltpu.HBM)
    updated = pl.pallas_call(
        kernel,
        out_shape=(jax.ShapeDtypeStruct((1024, K), BF16), jax.ShapeDtypeStruct((K, 1024), BF16)),
        in_specs=[hbm] * 4,
        out_specs=(pl.BlockSpec(memory_space=pltpu.VMEM), pl.BlockSpec(memory_space=pl.ANY)),
        scratch_shapes=scratch + sems,
        compiler_params=pltpu.CompilerParams(
            collective_id=0, has_side_effects=True, vmem_limit_bytes=32 * 1024 * 1024
        ),
    )(*(pltpu.with_memory_space_constraint(a, pltpu.HBM) for a in (tfidf, pattern, factor_w, factor_h)))
    return pl.pallas_call(
        write_out,
        out_shape=(jax.ShapeDtypeStruct((1024, K), BF16), jax.ShapeDtypeStruct((K, 1024), BF16)),
        in_specs=[pl.BlockSpec(memory_space=pl.ANY)] * 2,
        out_specs=(pl.BlockSpec(memory_space=pl.ANY),) * 2,
        scratch_shapes=[D((2,))],
    )(*(pltpu.with_memory_space_constraint(a, pltpu.VMEM) for a in updated))


def write_out(w, h, outw, outh, sem):
    copies = [pltpu.make_async_copy(w, outw, sem.at[0]), pltpu.make_async_copy(h, outh, sem.at[1])]
    for copy in copies:
        copy.start()
    for copy in copies:
        copy.wait()


def solution(mesh):
    placed = (P("term", "doc"), P("term", "doc"), P("term", None), P(None, "doc"))
    return jax.shard_map(
        on_device,
        mesh=mesh,
        in_specs=placed,
        out_specs=(P("term", None), P(None, "doc")),
        check_vma=False,
    )
```

```python
import jax
import jax.numpy as jnp
from jax import lax
from jax.experimental import pallas as pl
from jax.experimental.pallas import tpu as pltpu
from jax.sharding import PartitionSpec as P

K = 256
BLOCK = 128
NXY = 8
NZ = 16
MESH = pl.DeviceIdType.MESH
F32 = jnp.float32
BF16 = jnp.bfloat16
I16 = jnp.int16
LEVELS = 65535.0
XY = ((2, 1), (2, 0), (1, 1), (3, 1), (1, 0), (3, 0), (0, 1))
ZS = (8, 7, 9, 6, 10, 5, 11, 4, 12, 3, 13, 2, 14, 1, 15)
NEAR = 9


def dot(a, b, dims):
    return lax.dot_general(a, b, (dims, ((), ())), preferred_element_type=F32)


def encode(value, peak):
    inv = jnp.where(peak > 0.0, LEVELS / peak, 0.0)
    return ((value * inv + 0.5).astype(jnp.int32) - 32768).astype(I16)


def decode(code, step):
    return (code.astype(jnp.int32) + 32768).astype(F32) * step


def kernel(
    tf_hbm, pat_hbm, w_hbm, h_hbm, outw, outh,
    tf, masked, pat, w, wt, h, newh, newht,
    hsend, hrecv, hcode, hcode_in, hstep, hstep_in,
    gsend, grecv, gcode, gcode_in, gstep, gstep_in, gram_w, gram_u,
    gpart, gxy_in, gz, gz_in, gfull, gram_h, ratio,
    wcode, wcode_in, wstep, wstep_in, acc, zsum, zsum_in, znum_in, tiles,
    gz_step, gz_step_in, zown, zstep, zstep_in, znum_step,
    ready1, ready2,
    load_s, store_s, core_s, core_r, x2_s, x2_r, gxy_s, gxy_r, gz_s, gz_r, gf_s, gf_r,
    wf_s, wf_r, wn_s, wn_r, ws_s, ws_r, zs_s, zs_r, zn_s, zn_r, on_s, on_r, of_s, of_r,
    gt_s, gt_r, zt_s, zt_r, zm_s, zm_r,
):
    doc = lax.axis_index("doc")
    term = lax.axis_index("term")
    z = lax.rem(doc, NZ)
    q = lax.div(doc, NZ)
    y, xl = lax.div(q, 2), lax.rem(q, 2)
    xh = lax.div(term, 2)
    c = lax.rem(term, 2)
    oc = 1 - c

    def at_term(t):
        return {"doc": doc, "term": t}

    y_at = [lax.rem(y + i, 4) * 2 for i in range(4)]
    x_at = [xl, 1 - xl]
    xy_at = {off: y_at[off[0]] + x_at[off[1]] for off in ((0, 0),) + XY}
    z_at = [z] + [lax.rem(z + k, NZ) for k in range(1, NZ)]
    tile_at = [lax.rem(z + s + 12, NZ) for s in range(NZ)]
    half_at = [lax.div(tile, 8) for tile in tile_at]
    row_at = [lax.rem(tile, 8) * 16 for tile in tile_at]
    slot_at = [lax.rem(tile + 20 - z, NZ) for tile in range(NZ)]

    def xy_of(off):
        return xy_at[off]

    def at_xy(p):
        return {"doc": p * NZ + z, "term": term}

    def at_z(k):
        return {"doc": q * NZ + z_at[k % NZ], "term": term}

    term_at = [term] + [lax.rem(term + k, 4) for k in range(1, 4)]
    spread_at = [lax.div(t, 2) * (2 * NXY) + lax.rem(t, 2) for t in term_at]
    gram_at = {(i, dt): xy_at[off] * 2 + spread_at[dt] for i, off in enumerate(XY + ((0, 0),)) for dt in range(4)}
    mine = gram_at[len(XY), 0]

    core = at_term(xh * 2 + oc)
    across = at_term((1 - xh) * 2 + c)
    sends = []

    def remote(src, dst, ssem, rsem, device):
        return pltpu.make_async_remote_copy(
            src_ref=src, dst_ref=dst, send_sem=ssem, recv_sem=rsem, device_id=device, device_id_type=MESH
        )

    def send(src, dst, ssem, rsem, device, incoming=None):
        copy = remote(src, dst, ssem, rsem, device)
        copy.start()
        sends.append(copy)
        if incoming is not None:
            landing, sem = incoming
            copy = remote(landing, landing, ssem, sem, device)
        return copy

    chunks = [oc * 2, oc * 2 + 1, c * 2, c * 2 + 1]
    cols = [pl.ds(pl.multiple_of(g * 256, 256), 256) for g in chunks]
    load_w = pltpu.make_async_copy(w_hbm, w, load_s.at[0])
    load_pat = pltpu.make_async_copy(pat_hbm, pat, load_s.at[1])
    load_h = pltpu.make_async_copy(h_hbm, h, load_s.at[2])
    load_tf = [pltpu.make_async_copy(tf_hbm.at[:, cols[i]], tf.at[:, cols[i]], load_s.at[3 + i]) for i in range(4)]
    load_w.start()
    load_pat.start()
    for copy in load_tf:
        copy.start()
    load_h.start()

    barrier = pltpu.get_barrier_semaphore()
    greeted = [across] + [at_z(k) for k in (-2, 2)] + [at_xy(xy_of((2, 0)))]
    greeted += [at_xy(xy_of(off)) for off in ((1, 0), (3, 0), (0, 1))] + [at_z(k) for k in (-1, 1)] + [core]
    for device in greeted:
        pl.semaphore_signal(barrier, inc=1, device_id=device, device_id_type=MESH)

    load_w.wait()
    wt[...] = w[...].T
    gsend[...] = dot(wt[...], w[...], ((1,), (0,))).reshape(2, 128, K)
    def mask(i):
        load_tf[i].wait()
        for a in range(8):
            for b in range(2):
                rows = pl.ds(a * BLOCK, BLOCK)
                at = pl.ds(pl.multiple_of(chunks[i] * 256 + b * BLOCK, BLOCK), BLOCK)
                on = pat[a, chunks[i] * 2 + b].astype(F32).astype(BF16)
                masked[rows, at] = tf[rows, at] * on

    def numerator_h(i):
        return dot(wt[...], masked[:, cols[i]], ((1,), (0,)))

    pl.semaphore_wait(barrier, len(greeted))
    for device in (at_z(-2), at_z(2), at_xy(xy_of((0, 1)))):
        pl.semaphore_signal(ready1, inc=1, device_id=device, device_id_type=MESH)

    g_copy = send(gsend.at[oc], grecv, core_s.at[0], core_r.at[0], core)
    load_pat.wait()
    mask(0)
    hsend[0] = numerator_h(0)
    h_copy = [send(hsend.at[0], hrecv.at[0], core_s.at[1], core_r.at[1], core)]
    mask(1)
    hsend[1] = numerator_h(1)
    h_copy.append(send(hsend.at[1], hrecv.at[1], core_s.at[2], core_r.at[2], core))

    g_copy.wait_recv()
    part = gsend[c] + grecv[...]
    left, right = part[:, :128], part[:, 128:]
    first = c == 0
    blocks = (jnp.where(first, left, right), jnp.where(first, right[:64], left.T[64:]))
    for i, block in enumerate(blocks):
        peak = jnp.max(block, axis=0, keepdims=True)
        gstep[i] = peak / LEVELS
        gcode[i * 128 : i * 128 + block.shape[0]] = encode(block, peak)
    gx = [
        send(gcode, gcode_in, x2_s.at[0], x2_r.at[0], across),
        send(gstep, gstep_in, x2_s.at[1], x2_r.at[1], across),
    ]
    hx = []
    for u in range(2):
        mask(2 + u)
        own = numerator_h(2 + u)
        h_copy[u].wait_recv()
        part = own + hrecv[u]
        peak = jnp.max(part, axis=0, keepdims=True)
        hstep[u] = peak / LEVELS
        hcode[u] = encode(part, peak)
        if u == 1:
            pl.semaphore_wait(ready1, 3)
            for k in (-4, 4):
                pl.semaphore_signal(ready2, inc=1, device_id=at_z(k), device_id_type=MESH)
        hx.append(send(hstep.at[u], hstep_in.at[u], x2_s.at[2 + u], x2_r.at[2 + u], across))
        hx.append(send(hcode.at[u], hcode_in.at[u], x2_s.at[4 + u], x2_r.at[4 + u], across))

    for copy in gx:
        copy.wait_recv()
    for i, at in enumerate((slice(0, 128), slice(128, 192))):
        gram_u[c, at] = (decode(gcode[at], gstep[i]) + decode(gcode_in[at], gstep_in[i])).astype(BF16)
    gw = send(gram_u.at[c], gram_u.at[c], core_s.at[3], core_r.at[3], core)
    load_h.wait()
    gw.wait_recv()
    for i in range(2):
        gram_w[i, :, i * 128 : i * 128 + 128] = gram_u[i, :128]
        upper = gram_u[i, 128:]
        gram_w[0, i * 64 : i * 64 + 64, 128:] = upper
    gram_w[1, :, :128] = gram_w[0, :, 128:].T
    stores = []
    nh = []
    for u in range(2):
        hv = h[:, cols[2 + u]]
        den = dot(gram_w[...].reshape(K, K), hv, ((1,), (0,)))
        hx[2 * u].wait_recv()
        hx[2 * u + 1].wait_recv()
        total = decode(hcode[u], hstep[u]) + decode(hcode_in[u], hstep_in[u])
        new = (hv.astype(F32) * total / den).astype(BF16)
        g = chunks[2 + u]
        newh[g] = new
        theirs = newh.at[chunks[u]]
        nh.append(send(newh.at[g], newh.at[g], core_s.at[4 + u], core_r.at[4 + u], core, (theirs, core_r.at[4 + u])))
        stores.append(pltpu.make_async_copy(newh.at[g], outh.at[:, cols[2 + u]], store_s.at[u]))
        newht[pl.ds(pl.multiple_of(g * 256, 256), 256), :] = new.T

    rows = pl.ds(pl.multiple_of(xh * 128, 128), 128)
    for i in range(2):
        gpart[i] = sum(
            dot(newh[chunks[2 + u], rows, :], newht[pl.ds(pl.multiple_of(chunks[2 + u] * 256, 256), 256), i * 128 : i * 128 + 128], ((1,), (0,)))
            for u in range(2)
        )
    gxy = []
    n = 0
    for off in XY + ((0, 0),):
        p = xy_of(off)
        for dc in range(2):
            if off == (0, 0) and dc == 0:
                continue
            tc = lax.rem(c + dc, 2)
            tile = gpart.at[tc, pl.ds(pl.multiple_of(p * 16, 16), 16)]
            gxy.append(
                send(tile, gxy_in.at[n], gxy_s.at[n], gxy_r.at[n], {"doc": p * NZ + z, "term": xh * 2 + tc})
            )
            n += 1

    half = pl.ds(pl.multiple_of(c * 512, 512), 512)
    for p in range(NXY):
        acc[p] = dot(masked[p * 128 : (p + 1) * 128, half], newht[half, :], ((1,), (0,)))

    for u in range(2):
        g = chunks[u]
        nh[u].wait_recv()
        newht[cols[u], :] = newh[g].T
        if u == 0:
            for p in range(NXY):
                acc[p] += dot(masked[p * 128 : (p + 1) * 128, cols[0]], newht[cols[0], :], ((1,), (0,)))
        stores.append(pltpu.make_async_copy(newh.at[g], outh.at[:, cols[u]], store_s.at[2 + u]))

    for p in range(NXY):
        value = acc[p] + dot(masked[p * 128 : (p + 1) * 128, cols[1]], newht[cols[1], :], ((1,), (0,)))
        acc[p] = value
        peak = jnp.max(value, axis=0, keepdims=True)
        code = encode(value, peak)
        step = peak / LEVELS
        for i in range(2):
            wstep[p, i] = step[:, i * 128 : (i + 1) * 128]
            for b in range(8):
                wcode[p, slot_at[i * 8 + b]] = code[b * 16 : (b + 1) * 16, i * 128 : (i + 1) * 128]
    wf, wn, ws = [], [], []
    for k, off in enumerate(XY):
        p = xy_of(off)
        ws.append(send(wstep.at[p], wstep_in.at[k], ws_s.at[k], ws_r.at[k], at_xy(p)))
        wf.append(send(wcode.at[p, NEAR:], wcode_in.at[k, NEAR:], wf_s.at[k], wf_r.at[k], at_xy(p)))
    for k, off in enumerate(XY):
        p = xy_of(off)
        wn.append(send(wcode.at[p, :NEAR], wcode_in.at[k, :NEAR], wn_s.at[k], wn_r.at[k], at_xy(p)))
    for copy in stores:
        copy.start()

    gsum = gpart[c, pl.ds(pl.multiple_of(q * 16, 16), 16), :]
    for n in range(15):
        gxy[n].wait_recv()
        gsum = gsum + gxy_in[n]
    peak = jnp.max(gsum, axis=0, keepdims=True)
    gz_step[...] = peak / LEVELS
    gz_step_in[z] = peak / LEVELS
    code = encode(gsum, peak)
    gz[...] = code
    gz_in[z] = code
    pl.semaphore_wait(ready2, 2)
    gzc = []
    for k in ZS:
        p = z_at[k]
        gzc.append(send(gz_step, gz_step_in.at[z], gt_s.at[k], gt_r.at[z], at_z(k), (gz_step_in.at[p], gt_r.at[p])))
        gzc.append(send(gz, gz_in.at[z], gz_s.at[k], gz_r.at[z], at_z(k), (gz_in.at[p], gz_r.at[p])))

    def sum_xy(slots):
        for s in slots:
            half = half_at[s]
            total = acc[q, pl.ds(pl.multiple_of(row_at[s], 16), 16), pl.ds(pl.multiple_of(half * 128, 128), 128)]
            for k in range(7):
                total = total + decode(wcode_in[k, s], wstep_in[k, half])
            if s == 4:
                zown[...] = total
                continue
            peak = jnp.max(total, axis=0, keepdims=True)
            zstep[s] = peak / LEVELS
            zsum[s] = encode(total, peak)

    zs, zt = {}, {}
    for k in range(7):
        ws[k].wait_recv()
        wf[k].wait_recv()
    sum_xy(range(NEAR, NZ))
    for k in ZS[:7]:
        s = (k + 4) % NZ
        zt[s] = send(zstep.at[s], zstep_in.at[s], zt_s.at[s], zt_r.at[s], at_z(k))
        zs[s] = send(zsum.at[s], zsum_in.at[s], zs_s.at[s], zs_r.at[s], at_z(k))
    for k in range(7):
        wn[k].wait_recv()
    sum_xy(range(NEAR))
    for k in ZS[7:]:
        s = (k + 4) % NZ
        zt[s] = send(zstep.at[s], zstep_in.at[s], zt_s.at[s], zt_r.at[s], at_z(k))
        zs[s] = send(zsum.at[s], zsum_in.at[s], zs_s.at[s], zs_r.at[s], at_z(k))

    for copy in reversed(gzc):
        copy.wait_recv()
    gsum = decode(gz_in[0], gz_step_in[0])
    for p in range(1, NZ):
        gsum = gsum + decode(gz_in[p], gz_step_in[p])
    gfull[mine] = gsum.astype(BF16)
    gf = []
    n = 0
    for p_i, off in enumerate(XY + ((0, 0),)):
        p = xy_of(off)
        for dt in (2, 3, 1, 0):
            if off == (0, 0) and dt == 0:
                continue
            t = term_at[dt]
            at = gram_at[p_i, dt]
            device = {"doc": p * NZ + z, "term": t}
            gf.append(send(gfull.at[mine], gfull.at[mine], gf_s.at[n], gf_r.at[mine], device, (gfull.at[at], gf_r.at[at])))
            n += 1

    total = zown[...]
    for s in range(NZ):
        if s != 4:
            zt[s].wait_recv()
            zs[s].wait_recv()
            total = total + decode(zsum_in[s], zstep_in[s])
    peak = jnp.max(total, axis=0, keepdims=True)
    znum_in[4] = encode(total, peak)
    znum_step[4] = peak / LEVELS
    zn, zm = {}, {}
    for k in ZS:
        s = (4 - k) % NZ
        zm[s] = send(znum_step.at[4], znum_step.at[s], zm_s.at[s], zm_r.at[s], at_z(k))
        zn[s] = send(znum_in.at[4], znum_in.at[s], zn_s.at[s], zn_r.at[s], at_z(k))

    for copy in reversed(gf):
        copy.wait_recv()
    for a in range(16):
        for i in range(2):
            gram_h[pl.ds(a * 16, 16), pl.ds(i * 128, 128)] = gfull[a * 2 + i]
    wrows = w[pl.ds(pl.multiple_of(q * 128, 128), 128), :]
    ratio[...] = wrows.astype(F32) / dot(wrows, gram_h[...], ((1,), (0,)))

    def spot(s):
        return pl.multiple_of(row_at[s], 16), pl.multiple_of(half_at[s] * 128, 128)

    def finish(slots):
        for s in slots:
            row, col = spot(s)
            tiles[q, s] = (ratio[pl.ds(row, 16), pl.ds(col, 128)] * decode(znum_in[s], znum_step[s])).astype(BF16)

    for s in range(NEAR):
        if s != 4:
            zm[s].wait_recv()
            zn[s].wait_recv()
    finish(range(NEAR))
    on, of = [], []
    for k, off in enumerate(XY):
        src = tiles.at[q, :NEAR]
        p = xy_of(off)
        on.append(send(src, src, on_s.at[k], on_r.at[q], at_xy(p), (tiles.at[p, :NEAR], on_r.at[p])))
    for s in range(NEAR, NZ):
        zm[s].wait_recv()
        zn[s].wait_recv()
    finish(range(NEAR, NZ))
    for k, off in enumerate(XY):
        src = tiles.at[q, NEAR:]
        p = xy_of(off)
        of.append(send(src, src, of_s.at[k], of_r.at[q], at_xy(p), (tiles.at[p, NEAR:], of_r.at[p])))

    def place(p, slots):
        for s in slots:
            row, col = spot(s)
            outw[pl.ds(pl.multiple_of(p * 128 + row, 16), 16), pl.ds(col, 128)] = tiles[p, s]

    place(q, range(NZ))
    for k, off in enumerate(XY):
        p = xy_of(off)
        on[k].wait_recv()
        place(p, range(NEAR))
    for k, off in enumerate(XY):
        p = xy_of(off)
        of[k].wait_recv()
        place(p, range(NEAR, NZ))
    for copy in sends:
        copy.wait_send()
    for copy in stores:
        copy.wait()


def on_device(tfidf, pattern, factor_w, factor_h):
    V = pltpu.VMEM
    scratch = [
        V((1024, 1024), BF16), V((1024, 1024), BF16), pltpu.SMEM((8, 8), jnp.int32),
        V((1024, K), BF16), V((K, 1024), BF16), V((K, 1024), BF16), V((4, K, 256), BF16), V((1024, K), BF16),
        V((2, K, 256), F32), V((2, K, 256), F32), V((2, K, 256), I16), V((2, K, 256), I16),
        V((2, 1, 256), F32), V((2, 1, 256), F32),
        V((2, 128, K), F32), V((128, K), F32), V((192, 128), I16), V((192, 128), I16), V((2, 1, 128), F32), V((2, 1, 128), F32),
        V((2, 128, K), BF16), V((2, 192, 128), BF16),
        V((2, 128, 128), F32), V((15, 16, 128), F32), V((16, 128), I16), V((NZ, 16, 128), I16),
        V((32, 16, 128), BF16), V((K, K), BF16), V((128, K), F32),
        V((NXY, NZ, 16, 128), I16), V((7, NZ, 16, 128), I16), V((NXY, 2, 1, 128), F32), V((7, 2, 1, 128), F32),
        V((NXY, 128, K), F32), V((NZ, 16, 128), I16), V((NZ, 16, 128), I16), V((NZ, 16, 128), I16),
        V((NXY, NZ, 16, 128), BF16),
        V((1, 128), F32), V((NZ, 1, 128), F32), V((16, 128), F32), V((NZ, 1, 128), F32), V((NZ, 1, 128), F32), V((NZ, 1, 128), F32),
    ]
    D = pltpu.SemaphoreType.DMA
    sems = [pltpu.SemaphoreType.REGULAR, pltpu.SemaphoreType.REGULAR, D((7,)), D((4,))]
    for a, b in ((6, 6), (6, 6), (15, 15), (NZ, NZ), (31, 32), (7, 7), (7, 7), (7, 7), (NZ, NZ), (NZ, NZ), (7, 8), (7, 8), (NZ, NZ), (NZ, NZ), (NZ, NZ)):
        sems += [D((a,)), D((b,))]
    hbm = pl.BlockSpec(memory_space=pltpu.HBM)
    updated = pl.pallas_call(
        kernel,
        out_shape=(jax.ShapeDtypeStruct((1024, K), BF16), jax.ShapeDtypeStruct((K, 1024), BF16)),
        in_specs=[hbm] * 4,
        out_specs=(pl.BlockSpec(memory_space=pltpu.VMEM), pl.BlockSpec(memory_space=pl.ANY)),
        scratch_shapes=scratch + sems,
        compiler_params=pltpu.CompilerParams(
            collective_id=0, has_side_effects=True, vmem_limit_bytes=32 * 1024 * 1024
        ),
    )(*(pltpu.with_memory_space_constraint(a, pltpu.HBM) for a in (tfidf, pattern, factor_w, factor_h)))
    return pl.pallas_call(
        write_out,
        out_shape=(jax.ShapeDtypeStruct((1024, K), BF16), jax.ShapeDtypeStruct((K, 1024), BF16)),
        in_specs=[pl.BlockSpec(memory_space=pl.ANY)] * 2,
        out_specs=(pl.BlockSpec(memory_space=pl.ANY),) * 2,
        scratch_shapes=[D((2,))],
    )(*(pltpu.with_memory_space_constraint(a, pltpu.VMEM) for a in updated))


def write_out(w, h, outw, outh, sem):
    copies = [pltpu.make_async_copy(w, outw, sem.at[0]), pltpu.make_async_copy(h, outh, sem.at[1])]
    for copy in copies:
        copy.start()
    for copy in copies:
        copy.wait()


def solution(mesh):
    placed = (P("term", "doc"), P("term", "doc"), P("term", None), P(None, "doc"))
    return jax.shard_map(
        on_device,
        mesh=mesh,
        in_specs=placed,
        out_specs=(P("term", None), P(None, "doc")),
        check_vma=False,
    )
```
